32 devices in a mesh: groups: 2 (over y), ctx: 4 (over z), head: 2 (over x), rep: 2 (over core).
Axes of the slice: x: 2, y: 2, z: 4, core: 2. Of those that a mesh axis runs over, the one named last changes fastest.
Arguments:
- kv_rows: bfloat16 [1536, 8, 256], P(('groups', 'ctx'), ('head', 'rep')), parts along dimension 0, may hold values from -8 to 8
- kv_scales: float32 [8, 2], replicated, may hold values from 0.004 to 0.04
- queries: bfloat16 [2, 512, 16384], P(None, ('groups', 'ctx'), ('head', 'rep')), parts along dimension 1, may hold values from -8 to 8
- shard_counts: int32 [8], P(('groups', 'ctx')), parts along dimension 0, may hold values from 1 to 192, 576 in all
- span_starts: int32 [4], P('groups'), parts along dimension 0, may hold values from 0 to 320
- block_slots: int32 [96], P('groups'), parts along dimension 0, may hold values from 0 to 47, each once
Outputs:
- attention: bfloat16 [2, 512, 16384], P(None, ('groups', 'ctx'), ('head', 'rep')), parts along dimension 1
- decode_cache: float32 [1536, 8, 256], P(('groups', 'ctx'), 'head'), parts along dimension 0
The draws below stay inside these ranges and needn't reach their ends.
There are 2 independent parts, one for each index of `groups`. The reference program is written for one: setup_inputs(seed, part) draws one part's arguments, and reference() takes and returns one part's arrays. A program takes and returns all parts, laid end to end along the dimension named above; an argument that names none is the same for every part. Nothing has to cross between parts.
Inputs may be any that keep to these rules, and one draw needn't show every extreme that they name: `shard_counts`: one shard is full. `block_slots`: each slot once.
All inputs are finite; a program needn't handle non-finite values.
Results may differ from the reference program's by a relative error of at most 0.0095.
Values may be sent and summed in bfloat16 or wider, within the bound.
No kernel may reach another device: no remote copies, remote signals or barrier semaphores. Data moves between devices by JAX's collectives and lax.ppermute only.
A program may use at most 128 MiB of HBM per device.

```python
import math
import jax
import jax.numpy as jnp
import numpy as np
from jax import lax

KVH = 8
QH = 128
HD = 128
TOK_DEV = 192
QBLOCKS = 2
BLK = 16
TOKENS = 768
VALID = 576
QC = 256
NBLK = 48
N_CTX = 4


def draw_kv_rows(key, part):
    key = jax.random.fold_in(key, 11)
    shape = (TOKENS, KVH, 2 * HD)
    values = jax.random.truncated_normal(key, -6.0, 6.0, shape, jnp.float32)
    return values.astype(jnp.bfloat16)


def draw_queries(key, part):
    key = jax.random.fold_in(key, 23)
    shape = (QBLOCKS, QC, QH * HD)
    values = jax.random.truncated_normal(key, -6.0, 6.0, shape, jnp.float32) * 0.12
    return values.astype(jnp.bfloat16)


def split_up(amount, total, reach, slope):
    loads = [(1 << 20) // math.isqrt(rank ** slope) + 1 for rank in range(2, amount + 1)]
    spare, given = total - reach - (amount - 1), [1] * (amount - 1)
    while spare > 0:
        free = [i for i in range(amount - 1) if given[i] < reach]
        whole, budget = sum([loads[i] for i in free]), spare
        for i in free:
            addition = min(reach - given[i], max(1, budget * loads[i] // whole), spare)
            given[i] = given[i] + addition
            spare = spare - addition
    return np.array([reach] + given)


def ragged_sizes(key, count, total, most, slope):
    if count == 2:
        one = jax.random.randint(key, (), max(1, total - most), min(most, total - 1) + 1)
        return jnp.stack([one, total - one])
    sizes = jnp.asarray(split_up(count, total, most, slope), jnp.int32)
    pairs = (count - 1) // 2
    source_of, taker = sizes[1:1 + 2 * pairs:2], sizes[2:2 + 2 * pairs:2]
    slack = jnp.minimum(source_of - 1, most - taker)
    moved = jax.random.randint(jax.random.fold_in(key, 1), (pairs,), 0, 1 << 20) % (slack + 1)
    sizes = sizes.at[1:1 + 2 * pairs:2].set(source_of - moved).at[2:2 + 2 * pairs:2].set(taker + moved)
    return sizes[jax.random.permutation(jax.random.fold_in(key, 2), count)]


def setup_inputs(seed: int = 0, part: int = 0) -> dict:
    splits = jax.random.split(jax.random.key(seed), 7)
    part_splits = jax.random.split(jax.random.fold_in(splits[6], part), 7)
    return {
        "kv_rows": draw_kv_rows(jax.random.fold_in(jax.random.fold_in(splits[6], part), 71), part),
        "kv_scales": jnp.clip(jnp.exp(jax.random.uniform(splits[1], (KVH, 2), jnp.float32, math.log(0.004), math.log(0.04))), 0.004, 0.04),
        "queries": draw_queries(jax.random.fold_in(jax.random.fold_in(splits[6], part), 71), part),
        "shard_counts": ragged_sizes(part_splits[3], N_CTX, VALID, TOK_DEV, 2).astype(jnp.int32),
        "span_starts": jax.random.randint(part_splits[4], (QBLOCKS,), 0, VALID - QC + 1).astype(jnp.int32),
        "block_slots": jax.random.permutation(part_splits[5], NBLK).astype(jnp.int32),
    }


def sign_matrix(order):
    index_col = jnp.arange(order, dtype=jnp.int32)
    shared = jnp.bitwise_and(index_col[:, None], index_col[None, :])
    parity = jnp.zeros((order, order), jnp.int32)
    for bit_pos in range(order.bit_length()):
        parity = parity + jnp.bitwise_and(jnp.right_shift(shared, bit_pos), 1)
    parity = jnp.bitwise_and(parity, 1)
    return (1 - 2 * parity).astype(jnp.bfloat16)

def quantize(kv_values, scales):
    tokens, head_count, row_width = kv_values.shape
    half_width = row_width // 2
    rotated = jnp.dot(kv_values.reshape(tokens * head_count * 2, half_width), sign_matrix(half_width), preferred_element_type=jnp.float32) * (1.0 / math.sqrt(half_width))
    rotated = rotated.reshape(tokens, head_count, 2, half_width) / scales[None, :, :, None]
    return jnp.clip(rotated, -448.0, 448.0).astype(jnp.bfloat16).reshape(tokens, head_count, row_width)

def dequantize(kv_codes, scales):
    tokens, head_count, row_width = kv_codes.shape
    expanded = kv_codes.reshape(tokens, head_count, 2, row_width // 2).astype(jnp.float32) * scales[None, :, :, None]
    return expanded.reshape(tokens, head_count, row_width)

def reference(kv_rows, kv_scales, queries, shard_counts, span_starts, block_slots):
    kv_codes = quantize(kv_rows, kv_scales)
    offsets = (jnp.cumsum(shard_counts) - shard_counts).astype(jnp.int32)
    row_ids = jnp.arange(TOKENS, dtype=jnp.int32)
    shard_id = row_ids // TOK_DEV
    within = row_ids % TOK_DEV
    is_valid = within < shard_counts[shard_id]
    key_pos = (offsets[shard_id] + within).astype(jnp.int32)
    group_size = QH // KVH
    results = []
    for query_set in range(QBLOCKS):
        query_pos = span_starts[query_set] + jnp.arange(QC, dtype=jnp.int32)
        counted = is_valid[None, :] & (key_pos[None, :] <= query_pos[:, None])

        def one_head(head_id):
            kv_head = head_id // group_size
            query_cols = lax.dynamic_slice_in_dim(queries[query_set], head_id * HD, HD, 1)
            key_codes = kv_codes[:, kv_head, :HD]
            value_codes = kv_codes[:, kv_head, HD:]
            scores = jnp.dot(query_cols, key_codes.T, preferred_element_type=jnp.float32) * kv_scales[kv_head, 0]
            scores = jnp.where(counted, scores, -jnp.inf)
            row_max = lax.optimization_barrier(jnp.max(scores, axis=1, keepdims=True))
            probs = jnp.where(counted, jnp.exp(scores - row_max), 0.0)
            row_sum = lax.optimization_barrier(jnp.sum(probs, axis=1, keepdims=True))
            weighted = jnp.dot(probs.astype(jnp.bfloat16), value_codes, preferred_element_type=jnp.float32)
            return (weighted * kv_scales[kv_head, 1] / row_sum).astype(jnp.bfloat16)
        per_head = lax.map(one_head, jnp.arange(QH, dtype=jnp.int32))
        results.append(jnp.transpose(per_head, (1, 0, 2)).reshape(QC, QH * HD))
    attention = jnp.stack(results)
    block_id = jnp.clip(key_pos // BLK, 0, NBLK - 1)
    slot_id = block_slots[block_id]
    target = jnp.where(is_valid, slot_id * BLK + key_pos % BLK, TOKENS).astype(jnp.int32)
    decode_cache = jnp.zeros((TOKENS, KVH, 2 * HD), jnp.float32).at[target].set(dequantize(kv_codes, kv_scales), mode='drop')
    return (attention, decode_cache)
```

```python
import functools
import math

import jax
import jax.numpy as jnp
from jax import lax
from jax.experimental import pallas as pl
from jax.experimental.pallas import tpu as pltpu
from jax.sharding import PartitionSpec as P

BLK = 16
FLOOR = -1e9
MASKED = -1e30
LOG2E = math.log2(math.e)
VMEM_LIMIT = 48 * 1024 * 1024
SMEM_SPEC = pl.BlockSpec(memory_space=pltpu.SMEM)
VMEM_SPEC = pl.BlockSpec(memory_space=pltpu.VMEM)


def sign_pair(width):
    half = width // 2
    row = lax.broadcasted_iota(jnp.int32, (width, width), 0)
    col = lax.broadcasted_iota(jnp.int32, (width, width), 1)
    parity = row & col & (half - 1)
    parity = parity ^ (parity >> 4)
    parity = parity ^ (parity >> 2)
    parity = (parity ^ (parity >> 1)) & 1
    same = (row >= half) == (col >= half)
    return jnp.where(same, (1 - 2 * parity).astype(jnp.float32), 0.0).astype(jnp.bfloat16)


def codes_of(rows_ref, scale_of, signs, rot_scr):
    tokens, heads, width = rows_ref.shape
    half = width // 2
    flat = rows_ref[...].reshape(tokens * heads, width)
    rotated = jnp.dot(flat, signs, preferred_element_type=jnp.float32)
    rotated = rotated * (1.0 / math.sqrt(half))
    for w in range(2):
        rot_scr[w] = rotated[:, w * half : (w + 1) * half]
    found = []
    for j in range(heads):
        parts = []
        for w in range(2):
            own = rot_scr[w, pl.ds(j, tokens, stride=heads), :] if heads > 1 else rot_scr[w]
            parts.append(jnp.clip(own / scale_of(j, w), -448.0, 448.0).astype(jnp.bfloat16))
        found.append(parts)
    return found


def page_places(slots_ref, ctx_id, tokens):
    pages = slots_ref.shape[1]
    row = lax.broadcasted_iota(jnp.int32, (tokens, pages), 0)
    page = lax.broadcasted_iota(jnp.int32, (tokens, pages), 1)
    slot = ctx_id * (tokens // BLK) + (row >> 4)
    place = (page * BLK + (row & (BLK - 1))).astype(jnp.float32)
    hit = jnp.broadcast_to(slots_ref[...], (tokens, pages)) == slot
    return jnp.sum(jnp.where(hit, place, 0.0), axis=1, keepdims=True)


def picker(place, offset, count, tokens):
    key = lax.broadcasted_iota(jnp.int32, (tokens, tokens), 1)
    key_pos = (key + offset).astype(jnp.float32)
    hit = (jnp.broadcast_to(place, (tokens, tokens)) == key_pos) & (key < count)
    return jnp.where(hit, 1.0, 0.0).astype(jnp.bfloat16)


def span_of(meta, steps, tokens):
    if len(meta) == 1:
        return [(meta[0][0, 0], meta[0][0, 1])]
    me = lax.axis_index("ctx")
    known = [meta[0][0], meta[1][0], meta[2][0]]
    known.append(tokens * 3 - known[0] - known[1] - known[2])
    spans = []
    for step in steps:
        ident = me ^ step
        offset = jnp.int32(0)
        for other in range(4):
            offset = offset + jnp.where((me ^ other) < ident, known[other], 0)
        spans.append((offset, known[step]))
    return spans


def attend_kernel(metas, steps, has_state, last, with_pages, *refs):
    refs = list(refs)
    meta = [refs.pop(0) for _ in range(metas)]
    start_ref, scale_ref, query_ref = refs.pop(0), refs.pop(0), refs.pop(0)
    rows_refs = [refs.pop(0) for _ in steps]
    state = [refs.pop(0) for _ in range(3)] if has_state else None
    slots_ref = refs.pop(0) if with_pages else None
    if last:
        out_ref = refs.pop(0)
    else:
        acc_out, sum_out, top_out = refs.pop(0), refs.pop(0), refs.pop(0)
    moved_out = refs.pop(0) if with_pages else None
    rot_scr, score_scr, prob_scr = refs

    tokens, heads, width = rows_refs[0].shape
    half = width // 2
    sets, rows, query_width = query_ref.shape
    group = query_width // half // heads
    shards = len(steps)
    ctx_id = lax.axis_index("ctx")
    first_head = (lax.axis_index("head") * lax.axis_size("rep") + lax.axis_index("rep")) * heads
    spans = span_of(meta, steps, tokens)

    def scale_of(j, which):
        return scale_ref[which, first_head + j]

    signs = sign_pair(width)
    per_shard = [codes_of(r, scale_of, signs, rot_scr) for r in rows_refs]

    def joined(j, w):
        parts = [found[j][w] for found in per_shard]
        return jnp.concatenate(parts, axis=0) if shards > 1 else parts[0]

    keys = [joined(j, 0) for j in range(heads)]
    ones = jnp.ones((shards * tokens, half), jnp.bfloat16)
    values = [jnp.concatenate([joined(j, 1), ones], axis=1) for j in range(heads)]
    row = lax.broadcasted_iota(jnp.int32, (rows, tokens), 0)
    key = lax.broadcasted_iota(jnp.int32, (rows, tokens), 1)
    for c in range(sets):
        base = start_ref[c] + ctx_id * rows
        parts = []
        for offset, count in spans:
            counted = (key < count) & (key + offset <= base + row)
            parts.append(jnp.where(counted, 0.0, MASKED))
        bias = jnp.concatenate(parts, axis=1) if shards > 1 else parts[0]
        for j in range(heads):
            factor = scale_of(j, 0) * LOG2E
            stacked = jnp.concatenate(
                [
                    query_ref[c, :, (j * group + g) * half : (j * group + g + 1) * half]
                    for g in range(group)
                ],
                axis=0,
            )
            slot = (c * heads + j) % 2
            score_scr[slot] = lax.dot_general(
                stacked, keys[j], (((1,), (1,)), ((), ())), preferred_element_type=jnp.float32
            )
            alphas = []
            for g in range(group):
                here = slice(g * rows, (g + 1) * rows)
                scores = score_scr[slot, here, :] + bias
                top = jnp.max(scores, axis=1, keepdims=True)
                if has_state:
                    before = state[2][c, j, here, :]
                    after = jnp.maximum(jnp.broadcast_to(top, before.shape), before)
                    alphas.append(jnp.exp2((before - after) * factor))
                    top = after[:, :1]
                else:
                    top = jnp.maximum(top, FLOOR)
                probs = jnp.exp2((scores - top) * factor)
                prob_scr[slot, here, :] = probs.astype(jnp.bfloat16)
                if not last:
                    top_out[c, j, here, :] = jnp.broadcast_to(top, (rows, half))
            weighted = jnp.dot(prob_scr[slot], values[j], preferred_element_type=jnp.float32)
            for g in range(group):
                h = j * group + g
                here = slice(g * rows, (g + 1) * rows)
                acc = weighted[here, :half]
                total = weighted[here, half:]
                if has_state:
                    acc = acc + state[0][c, j, here, :] * alphas[g]
                    total = total + state[1][c, j, here, :] * alphas[g]
                if last:
                    result = acc * scale_of(j, 1) / total
                    out_ref[c, :, h * half : (h + 1) * half] = result.astype(jnp.bfloat16)
                else:
                    acc_out[c, j, here, :] = acc
                    sum_out[c, j, here, :] = total

    if with_pages:
        place = page_places(slots_ref, ctx_id, tokens)
        total = None
        for (offset, count), found in zip(spans, per_shard):
            pick = picker(place, offset, count, tokens)
            own = jnp.concatenate([part for parts in found for part in parts], axis=1)
            part = jnp.dot(pick, own, preferred_element_type=jnp.float32)
            total = part if total is None else total + part
        moved_out[...] = total.astype(jnp.bfloat16)


def attend(meta, steps, starts, scales, query, rows, state=None, last=False, slots=None):
    tokens, heads, width = rows[0].shape
    half = width // 2
    sets, query_rows, query_width = query.shape
    group = query_width // half // heads
    args = [*meta, starts, scales, query, *rows]
    specs = [SMEM_SPEC] * (len(meta) + 2) + [VMEM_SPEC] * (1 + len(rows))
    if state is not None:
        args += list(state)
        specs += [VMEM_SPEC] * 3
    if slots is not None:
        args.append(slots)
        specs.append(VMEM_SPEC)
    stacked = (sets, heads, group * query_rows, half)
    if last:
        outs = [jax.ShapeDtypeStruct(query.shape, jnp.bfloat16)]
    else:
        outs = [jax.ShapeDtypeStruct(stacked, jnp.float32)] * 3
    if slots is not None:
        outs.append(jax.ShapeDtypeStruct((tokens, heads * width), jnp.bfloat16))
    keys = tokens * len(rows)
    work = sets * heads * group * query_rows * keys
    return pl.pallas_call(
        functools.partial(
            attend_kernel, len(meta), steps, state is not None, last, slots is not None
        ),
        out_shape=outs,
        in_specs=specs,
        out_specs=[VMEM_SPEC] * len(outs),
        scratch_shapes=[
            pltpu.VMEM((2, tokens * heads, half), jnp.float32),
            pltpu.VMEM((2, group * query_rows, keys), jnp.float32),
            pltpu.VMEM((2, group * query_rows, keys), jnp.bfloat16),
        ],
        compiler_params=pltpu.CompilerParams(vmem_limit_bytes=VMEM_LIMIT),
        cost_estimate=pl.CostEstimate(
            flops=work * half * 8, bytes_accessed=4 << 20, transcendentals=work
        ),
    )(*args)


def cache_kernel(metas, steps, *refs):
    refs = list(refs)
    meta = [refs.pop(0) for _ in range(metas)]
    scale_ref, slots_ref, own, other, own_rows, other_rows, out_ref, rot_scr = refs
    tokens, heads, width = own_rows.shape
    half = width // 2
    ctx_id = lax.axis_index("ctx")
    rep_id = lax.axis_index("rep")
    pair_head = lax.axis_index("head") * lax.axis_size("rep") * heads
    signs = sign_pair(width)
    place = page_places(slots_ref, ctx_id, tokens)
    ((offset, count),) = span_of(meta, steps, tokens)
    pick = picker(place, offset, count, tokens)

    for turn in range(2):

        @pl.when(rep_id == turn)
        def _(turn=turn):
            for first, moved, rows in (
                (turn * heads, own, own_rows),
                ((1 - turn) * heads, other, other_rows),
            ):

                def scale_of(j, w, first=first):
                    return scale_ref[w, pair_head + first + j]

                found = codes_of(rows, scale_of, signs, rot_scr)
                for j in range(heads):
                    for w in range(2):
                        here = slice((2 * j + w) * half, (2 * j + w + 1) * half)
                        full = jnp.dot(pick, found[j][w], preferred_element_type=jnp.float32)
                        full = (full + moved[:, here].astype(jnp.float32)) * scale_of(j, w)
                        out_ref[:, first + j, w * half : (w + 1) * half] = full


def fill_cache(meta, steps, scales, slots, own, other, own_rows, other_rows):
    tokens, heads, width = own_rows.shape
    return pl.pallas_call(
        functools.partial(cache_kernel, len(meta), steps),
        out_shape=jax.ShapeDtypeStruct((tokens, 2 * heads, width), jnp.float32),
        in_specs=[SMEM_SPEC] * (len(meta) + 1) + [VMEM_SPEC] * 5,
        out_specs=VMEM_SPEC,
        scratch_shapes=[pltpu.VMEM((2, tokens * heads, width // 2), jnp.float32)],
        compiler_params=pltpu.CompilerParams(vmem_limit_bytes=VMEM_LIMIT),
        cost_estimate=pl.CostEstimate(
            flops=tokens * tokens * heads * width * 8, bytes_accessed=2 << 20, transcendentals=0
        ),
    )(*meta, scales, slots, own, other, own_rows, other_rows)


def pair(value, axis, step):
    size = lax.axis_size(axis)
    return lax.ppermute(value, axis, [(i, i ^ step) for i in range(size)])


def body(kv_rows, kv_scales, queries, shard_counts, span_starts, block_slots):
    scales = kv_scales.T
    slots = block_slots[None, :]
    across = pair(kv_rows, "ctx", 2)
    beside = pair(kv_rows, "ctx", 1)
    meta = [shard_counts, pair(shard_counts, "ctx", 1), pair(shard_counts, "ctx", 2)]
    corner = pair(across, "ctx", 1)
    *state, moved = attend(
        meta, (0, 1, 2), span_starts, scales, queries, [kv_rows, beside, across], slots=slots
    )
    moved_other = pair(moved, "rep", 1)
    corner_other = pair(corner, "rep", 1)
    (attention,) = attend(meta, (3,), span_starts, scales, queries, [corner], state, last=True)
    decode_cache = fill_cache(
        meta, (3,), scales, slots, moved, moved_other, corner, corner_other
    )
    return attention, decode_cache


def body_any(kv_rows, kv_scales, queries, shard_counts, span_starts, block_slots):
    tokens, heads, width = kv_rows.shape
    sets, query_rows, query_width = queries.shape
    half = width // 2
    group = query_width // half // heads
    scales = kv_scales.T
    slots = block_slots[None, :]
    counts = lax.all_gather(shard_counts, "ctx", axis=0, tiled=True)
    info = jnp.stack([jnp.cumsum(counts) - counts, counts], axis=1)
    every = lax.all_gather(kv_rows, "ctx", axis=0)

    def step(carry, turn):
        state, moved = carry
        rows, one = turn
        *state, found = attend(
            [one[None]], (0,), span_starts, scales, queries, [rows], state, slots=slots
        )
        return (tuple(state), moved + found), None

    stacked = (sets, heads, group * query_rows, half)
    state = (
        jnp.zeros(stacked, jnp.float32),
        jnp.zeros(stacked, jnp.float32),
        jnp.full(stacked, FLOOR, jnp.float32),
    )
    moved = jnp.zeros((tokens, heads * width), jnp.bfloat16)
    (state, moved), _ = lax.scan(step, (state, moved), (every[:-1], info[:-1]))
    attention, found = attend(
        [info[-1:]], (0,), span_starts, scales, queries, [every[-1]], state, last=True, slots=slots
    )
    moved = moved + found
    none = jnp.zeros((1, 2), jnp.int32)
    decode_cache = fill_cache(
        [none], (0,), scales, slots, moved, pair(moved, "rep", 1), kv_rows, kv_rows
    )
    return attention, decode_cache


def solution(mesh):
    in_specs = (
        P(("groups", "ctx"), ("head", "rep"), None),
        P(),
        P(None, ("groups", "ctx"), ("head", "rep")),
        P(("groups", "ctx")),
        P("groups"),
        P("groups"),
    )
    out_specs = (P(None, ("groups", "ctx"), ("head", "rep")), P(("groups", "ctx"), "head", None))
    chosen = body if mesh.shape["ctx"] == 4 else body_any
    return jax.shard_map(chosen, mesh=mesh, in_specs=in_specs, out_specs=out_specs, check_vma=False)
```

```python
import functools
import math

import jax
import jax.numpy as jnp
from jax import lax
from jax.experimental import pallas as pl
from jax.experimental.pallas import tpu as pltpu
from jax.sharding import PartitionSpec as P

BLK = 16
FLOOR = -1e9
MASKED = -1e30
TINY = 1e-30
LOG2E = math.log2(math.e)
VMEM_LIMIT = 48 * 1024 * 1024
SMEM_SPEC = pl.BlockSpec(memory_space=pltpu.SMEM)
VMEM_SPEC = pl.BlockSpec(memory_space=pltpu.VMEM)


def sign_pair(width):
    half = width // 2
    row = lax.broadcasted_iota(jnp.int32, (width, width), 0)
    col = lax.broadcasted_iota(jnp.int32, (width, width), 1)
    parity = row & col & (half - 1)
    parity = parity ^ (parity >> 4)
    parity = parity ^ (parity >> 2)
    parity = (parity ^ (parity >> 1)) & 1
    same = (row >= half) == (col >= half)
    return jnp.where(same, (1 - 2 * parity).astype(jnp.float32), 0.0).astype(jnp.bfloat16)


def codes_of(rows_ref, scale_of, signs, rot_scr):
    tokens, heads, width = rows_ref.shape
    half = width // 2
    flat = rows_ref[...].reshape(tokens * heads, width)
    rotated = jnp.dot(flat, signs, preferred_element_type=jnp.float32)
    rotated = rotated * (1.0 / math.sqrt(half))
    for w in range(2):
        rot_scr[w] = rotated[:, w * half : (w + 1) * half]
    found = []
    for j in range(heads):
        parts = []
        for w in range(2):
            own = rot_scr[w, pl.ds(j, tokens, stride=heads), :] if heads > 1 else rot_scr[w]
            parts.append(jnp.clip(own / scale_of(j, w), -448.0, 448.0).astype(jnp.bfloat16))
        found.append(parts)
    return found


def page_places(slots_ref, ctx_id, tokens):
    pages = slots_ref.shape[1]
    row = lax.broadcasted_iota(jnp.int32, (tokens, pages), 0)
    page = lax.broadcasted_iota(jnp.int32, (tokens, pages), 1)
    slot = ctx_id * (tokens // BLK) + (row >> 4)
    place = (page * BLK + (row & (BLK - 1))).astype(jnp.float32)
    hit = jnp.broadcast_to(slots_ref[...], (tokens, pages)) == slot
    return jnp.sum(jnp.where(hit, place, 0.0), axis=1, keepdims=True)


def picker(distance, offset, count):
    key = lax.broadcasted_iota(jnp.int32, distance.shape, 1)
    hit = (distance == offset.astype(jnp.float32)) & (key < count)
    return jnp.where(hit, 1.0, 0.0).astype(jnp.bfloat16)


def spans_of(count_refs, info_ref, steps, tokens):
    if info_ref is not None:
        return [(info_ref[0, 0], info_ref[0, 1])]
    me = lax.axis_index("ctx")
    known = [ref[0:1, :][0, 0] for ref in count_refs]
    known.append(tokens * 3 - known[0] - known[1] - known[2])
    spans = []
    for step in steps:
        ident = me ^ step
        offset = jnp.int32(0)
        for other in range(4):
            offset = offset + jnp.where((me ^ other) < ident, known[other], 0)
        spans.append((offset, known[step]))
    return spans


def ready_kernel(*refs):
    sources, refs = refs[:6], refs[6:]
    ints_out, floats_out, signs_out, place_out, codes_out, query_ref, rot_scr = refs[:7]
    start_ref, scale_ref, count_ref, slots_ref, rows_ref, sems = refs[7:]
    held = (start_ref, scale_ref, count_ref, slots_ref, rows_ref, query_ref)
    copies = [pltpu.make_async_copy(a, b, sems.at[i]) for i, (a, b) in enumerate(zip(sources, held))]
    for copy in copies:
        copy.start()
    tokens, heads, width = rows_ref.shape
    sets, rows, _ = query_ref.shape
    ctx_id = lax.axis_index("ctx")
    rep_id = lax.axis_index("rep")
    pair_head = lax.axis_index("head") * lax.axis_size("rep") * heads
    signs = sign_pair(width)
    signs_out[...] = signs
    ints_out[...] = jnp.zeros(ints_out.shape, jnp.int32)
    floats_out[...] = jnp.zeros(floats_out.shape, jnp.float32)
    for copy in copies[:5]:
        copy.wait()
    ints_out[0:1, :] = jnp.full((1, 128), count_ref[0], jnp.int32)
    for c in range(sets):
        ints_out[1 + c : 2 + c, :] = jnp.full((1, 128), start_ref[c] + ctx_id * rows, jnp.int32)
    for side, member in enumerate((rep_id, 1 - rep_id)):
        for j in range(heads):
            for w in range(2):
                scale = scale_ref[w, pair_head + member * heads + j]
                at = (side * heads + j) * 2 + w
                floats_out[at : at + 1, :] = jnp.full((1, 128), scale, jnp.float32)
    place = jnp.broadcast_to(page_places(slots_ref, ctx_id, tokens), (tokens, tokens))
    token = lax.broadcasted_iota(jnp.int32, (tokens, tokens), 1)
    place_out[...] = place - token.astype(jnp.float32)
    found = codes_of(rows_ref, scale_reader(floats_out, 0, heads), signs, rot_scr)
    codes_out[...] = jnp.concatenate([part for parts in found for part in parts], axis=1)
    copies[5].wait()


def scale_reader(floats_ref, side, heads):
    def scale_of(j, w):
        at = (side * heads + j) * 2 + w
        return floats_ref[at : at + 1, :]

    return scale_of


def make_ready(starts, scales, counts, slots, rows, query):
    tokens, heads, width = rows.shape
    half = width // 2
    return pl.pallas_call(
        ready_kernel,
        out_shape=[
            jax.ShapeDtypeStruct((8, 128), jnp.int32),
            jax.ShapeDtypeStruct((8, 128), jnp.float32),
            jax.ShapeDtypeStruct((width, width), jnp.bfloat16),
            jax.ShapeDtypeStruct((tokens, tokens), jnp.float32),
            jax.ShapeDtypeStruct((tokens, heads * width), jnp.bfloat16),
            jax.ShapeDtypeStruct(query.shape, query.dtype),
        ],
        in_specs=[pl.BlockSpec(memory_space=pltpu.HBM)] * 6,
        out_specs=[VMEM_SPEC] * 6,
        scratch_shapes=[
            pltpu.VMEM((2, tokens * heads, half), jnp.float32),
            pltpu.SMEM(starts.shape, jnp.int32),
            pltpu.SMEM(scales.shape, jnp.float32),
            pltpu.SMEM(counts.shape, jnp.int32),
            pltpu.VMEM(slots.shape, jnp.int32),
            pltpu.VMEM(rows.shape, rows.dtype),
            pltpu.SemaphoreType.DMA((6,)),
        ],
        compiler_params=pltpu.CompilerParams(vmem_limit_bytes=VMEM_LIMIT),
        cost_estimate=pl.CostEstimate(
            flops=tokens * heads * width * width * 2, bytes_accessed=2 << 20, transcendentals=0
        ),
    )(starts, scales, counts, slots, rows, query)


def attend_kernel(metas, steps, with_codes, has_state, last, with_pages, *refs):
    refs = list(refs)
    info_ref = refs.pop(0) if metas == 0 else None
    count_refs = [refs.pop(0) for _ in range(metas)]
    ints_ref, floats_ref, signs_ref, query_ref = [refs.pop(0) for _ in range(4)]
    codes_ref = refs.pop(0) if with_codes else None
    rows_refs = [refs.pop(0) for _ in range(len(steps) - with_codes)]
    state = [refs.pop(0) for _ in range(2)] if has_state else None
    place_ref = refs.pop(0) if with_pages else None
    out_ref = refs.pop(0)
    level_out = None if last else refs.pop(0)
    moved_out = refs.pop(0) if with_pages else None
    rot_scr = refs.pop(0)

    tokens, heads, width = rows_refs[0].shape
    half = width // 2
    sets, rows, query_width = query_ref.shape
    group = query_width // half // heads
    stack = group * rows
    shards = len(steps)
    spans = spans_of(count_refs, info_ref, steps, tokens)
    bases = [ints_ref[1 + c : 2 + c, :][0, 0] for c in range(sets)]
    scale_of = scale_reader(floats_ref, 0, heads)
    if last:
        outs, sems = refs

    def finish(c, j):
        here = pl.ds(j * group * half, group * half)
        return pltpu.make_async_copy(outs.at[c, :, here], out_ref.at[c, :, here], sems.at[c * heads + j])

    def compute():
        signs = signs_ref[...]
        per_shard = []
        if with_codes:
            per_shard.append(
                [
                    [codes_ref[:, (2 * j + w) * half : (2 * j + w + 1) * half] for w in range(2)]
                    for j in range(heads)
                ]
            )
        per_shard += [codes_of(r, scale_of, signs, rot_scr) for r in rows_refs]

        def joined(j, w):
            parts = [found[j][w] for found in per_shard]
            return jnp.concatenate(parts, axis=0) if shards > 1 else parts[0]

        keys = [joined(j, 0) for j in range(heads)]
        ones = jnp.ones((shards * tokens, half), jnp.bfloat16)
        values = [jnp.concatenate([joined(j, 1), ones], axis=1) for j in range(heads)]
        row = lax.broadcasted_iota(jnp.int32, (rows, tokens), 0)
        key = lax.broadcasted_iota(jnp.int32, (rows, tokens), 1)
        for c in range(sets):
            parts = []
            for offset, count in spans:
                counted = (key < count) & (key + (offset - bases[c]) <= row)
                parts.append(jnp.where(counted, 0.0, MASKED))
            bias = jnp.concatenate(parts, axis=1) if shards > 1 else parts[0]
            bias = jnp.concatenate([bias] * group, axis=0)
            for j in range(heads):
                factor = scale_of(j, 0) * LOG2E
                stacked = jnp.concatenate(
                    [
                        query_ref[c, :, (j * group + g) * half : (j * group + g + 1) * half]
                        for g in range(group)
                    ],
                    axis=0,
                )
                scores = lax.dot_general(
                    stacked, keys[j], (((1,), (1,)), ((), ())), preferred_element_type=jnp.float32
                )
                scores = scores + bias
                top = jnp.max(scores, axis=1, keepdims=True)
                top = jnp.broadcast_to(top, (stack, half))
                if has_state:
                    level = state[1][c, j]
                    top = jnp.maximum(top, level)
                else:
                    top = jnp.maximum(top, FLOOR)
                probs = []
                for i in range(0, scores.shape[1], half):
                    part = scores[:, i : min(i + half, scores.shape[1])]
                    size = part.shape[1]
                    part = jnp.exp2((part - top[:, :size]) * factor[:, :size])
                    probs.append(part.astype(jnp.bfloat16))
                weighted = jnp.dot(
                    jnp.concatenate(probs, axis=1), values[j], preferred_element_type=jnp.float32
                )
                acc = weighted[:, :half] * scale_of(j, 1)
                total = weighted[:, half:]
                if has_state:
                    alpha = jnp.exp2((level - top) * factor)
                    total = total + alpha
                else:
                    total = jnp.maximum(total, TINY)
                target = outs if last else out_ref
                for g in range(group):
                    one = slice(g * rows, (g + 1) * rows)
                    cols = slice((j * group + g) * half, (j * group + g + 1) * half)
                    part = acc[one]
                    if has_state:
                        part = part + state[0][c, :, cols].astype(jnp.float32) * alpha[one]
                    target[c, :, cols] = (part / total[one]).astype(jnp.bfloat16)
                if last:
                    finish(c, j).start()
                else:
                    level_out[c, j] = top + jnp.log2(total) / factor
        if last:
            for c in range(sets):
                for j in range(heads):
                    finish(c, j).wait()
        return per_shard

    if last:
        latest = bases[0]
        for base in bases[1:]:
            latest = jnp.maximum(latest, base)
        needed = spans[0][0] < latest + rows

        @pl.when(needed)
        def _():
            compute()

        @pl.when(jnp.logical_not(needed))
        def _():
            whole = pltpu.make_async_copy(state[0], out_ref, sems.at[0])
            whole.start()
            whole.wait()

    else:
        per_shard = compute()
    if with_pages:
        place = place_ref[...]
        total = None
        for (offset, count), found in zip(spans, per_shard):
            pick = picker(place, offset, count)
            own = jnp.concatenate([part for parts in found for part in parts], axis=1)
            part = jnp.dot(pick, own, preferred_element_type=jnp.float32)
            total = part if total is None else total + part
        moved_out[...] = total.astype(jnp.bfloat16)


def attend(counts, info, steps, ready, rows, codes=None, state=None, last=False):
    ints, floats, signs, place, _, query = ready
    tokens, heads, width = rows[0].shape
    half = width // 2
    sets, query_rows, query_width = query.shape
    group = query_width // half // heads
    args = list(counts) if info is None else [info]
    specs = [VMEM_SPEC] * len(counts) if info is None else [SMEM_SPEC]
    args += [ints, floats, signs, query]
    if codes is not None:
        args.append(codes)
    args += rows
    if state is not None:
        args += list(state)
    if not last:
        args.append(place)
    specs += [VMEM_SPEC] * (len(args) - len(specs))
    outs = [jax.ShapeDtypeStruct(query.shape, jnp.bfloat16)]
    out_specs = [pl.BlockSpec(memory_space=pl.ANY) if last else VMEM_SPEC]
    scratch = [pltpu.VMEM((2, tokens * heads, half), jnp.float32)]
    if last:
        scratch += [
            pltpu.VMEM(query.shape, jnp.bfloat16),
            pltpu.SemaphoreType.DMA((sets * heads,)),
        ]
    else:
        outs += [
            jax.ShapeDtypeStruct((sets, heads, group * query_rows, half), jnp.float32),
            jax.ShapeDtypeStruct((tokens, heads * width), jnp.bfloat16),
        ]
        out_specs += [VMEM_SPEC] * 2
    keys = tokens * len(steps)
    work = sets * heads * group * query_rows * keys
    return pl.pallas_call(
        functools.partial(
            attend_kernel,
            len(counts) if info is None else 0,
            steps,
            codes is not None,
            state is not None,
            last,
            not last,
        ),
        out_shape=outs,
        in_specs=specs,
        out_specs=out_specs,
        scratch_shapes=scratch,
        compiler_params=pltpu.CompilerParams(vmem_limit_bytes=VMEM_LIMIT),
        cost_estimate=pl.CostEstimate(
            flops=work * half * 8, bytes_accessed=4 << 20, transcendentals=work
        ),
    )(*args)


def cache_kernel(metas, steps, *refs):
    refs = list(refs)
    info_ref = refs.pop(0) if metas == 0 else None
    count_refs = [refs.pop(0) for _ in range(metas)]
    floats_ref, signs_ref, place_ref, own, other, own_rows, other_rows, out_ref, rot_scr = refs
    tokens, heads, width = own_rows.shape
    half = width // 2
    rep_id = lax.axis_index("rep")
    signs = signs_ref[...]
    ((offset, count),) = spans_of(count_refs, info_ref, steps, tokens)
    pick = picker(place_ref[...], offset, count)
    full = []
    for side, (moved, rows) in enumerate(((own, own_rows), (other, other_rows))):
        scale_of = scale_reader(floats_ref, side, heads)
        found = codes_of(rows, scale_of, signs, rot_scr)
        for j in range(heads):
            for w in range(2):
                here = slice((2 * j + w) * half, (2 * j + w + 1) * half)
                part = jnp.dot(pick, found[j][w], preferred_element_type=jnp.float32)
                full.append((part + moved[:, here].astype(jnp.float32)) * scale_of(j, w))

    for turn in range(2):

        @pl.when(rep_id == turn)
        def _(turn=turn):
            for side in range(2):
                first = (side if turn == 0 else 1 - side) * heads
                for j in range(heads):
                    for w in range(2):
                        value = full[(side * heads + j) * 2 + w]
                        out_ref[:, first + j, w * half : (w + 1) * half] = value


def fill_cache(counts, info, steps, ready, own, other, own_rows, other_rows):
    _, floats, signs, place, _, _ = ready
    tokens, heads, width = own_rows.shape
    args = list(counts) if info is None else [info]
    specs = [VMEM_SPEC] * len(counts) if info is None else [SMEM_SPEC]
    args += [floats, signs, place, own, other, own_rows, other_rows]
    specs += [VMEM_SPEC] * 7
    return pl.pallas_call(
        functools.partial(cache_kernel, len(counts) if info is None else 0, steps),
        out_shape=jax.ShapeDtypeStruct((tokens, 2 * heads, width), jnp.float32),
        in_specs=specs,
        out_specs=VMEM_SPEC,
        scratch_shapes=[pltpu.VMEM((2, tokens * heads, width // 2), jnp.float32)],
        compiler_params=pltpu.CompilerParams(vmem_limit_bytes=VMEM_LIMIT),
        cost_estimate=pl.CostEstimate(
            flops=tokens * tokens * heads * width * 8, bytes_accessed=2 << 20, transcendentals=0
        ),
    )(*args)


def pair(value, axis, step):
    size = lax.axis_size(axis)
    return lax.ppermute(value, axis, [(i, i ^ step) for i in range(size)])


def body(kv_rows, kv_scales, queries, shard_counts, span_starts, block_slots):
    across = pair(kv_rows, "ctx", 2)
    beside = pair(kv_rows, "ctx", 1)
    ready = make_ready(
        span_starts, kv_scales.T, shard_counts, block_slots[None, :], kv_rows, queries
    )
    count = jnp.broadcast_to(shard_counts[:, None], (8, 128))
    counts = [count, pair(count, "ctx", 1), pair(count, "ctx", 2)]
    corner = pair(across, "ctx", 1)
    *state, moved = attend(counts, None, (0, 1, 2), ready, [beside, across], ready[4])
    moved_other = pair(moved, "rep", 1)
    corner_other = pair(corner, "rep", 1)
    (attention,) = attend(counts, None, (3,), ready, [corner], None, state, True)
    decode_cache = fill_cache(
        counts, None, (3,), ready, moved, moved_other, corner, corner_other
    )
    return attention, decode_cache


def body_any(kv_rows, kv_scales, queries, shard_counts, span_starts, block_slots):
    counts = lax.all_gather(shard_counts, "ctx", axis=0, tiled=True)
    info = jnp.stack([jnp.cumsum(counts) - counts, counts], axis=1)
    every = lax.all_gather(kv_rows, "ctx", axis=0)
    ready = make_ready(
        span_starts, kv_scales.T, shard_counts, block_slots[None, :], kv_rows, queries
    )

    def step(carry, turn):
        state, moved = carry
        rows, one = turn
        *state, found = attend([], one[None], (0,), ready, [rows], None, state)
        return (tuple(state), moved + found), None

    *state, moved = attend([], info[:1], (0,), ready, [every[0]])
    (state, moved), _ = lax.scan(step, (tuple(state), moved), (every[1:], info[1:]))
    none = jnp.zeros((1, 2), jnp.int32)
    decode_cache = fill_cache(
        [], none, (0,), ready, moved, pair(moved, "rep", 1), kv_rows, kv_rows
    )
    return state[0], decode_cache


def solution(mesh):
    in_specs = (
        P(("groups", "ctx"), ("head", "rep"), None),
        P(),
        P(None, ("groups", "ctx"), ("head", "rep")),
        P(("groups", "ctx")),
        P("groups"),
        P("groups"),
    )
    out_specs = (P(None, ("groups", "ctx"), ("head", "rep")), P(("groups", "ctx"), "head", None))
    chosen = body if mesh.shape["ctx"] == 4 else body_any
    return jax.shard_map(chosen, mesh=mesh, in_specs=in_specs, out_specs=out_specs, check_vma=False)
```

```python
import functools
import math

import jax
import jax.numpy as jnp
from jax import lax
from jax.experimental import pallas as pl
from jax.experimental.pallas import tpu as pltpu
from jax.sharding import PartitionSpec as P

BLK = 16
FLOOR = -1e9
MASKED = -1e30
TINY = 1e-30
PIECES = 4
LOG2E = math.log2(math.e)
VMEM_LIMIT = 48 * 1024 * 1024
SMEM_SPEC = pl.BlockSpec(memory_space=pltpu.SMEM)
VMEM_SPEC = pl.BlockSpec(memory_space=pltpu.VMEM)


def sign_pair(width):
    half = width // 2
    row = lax.broadcasted_iota(jnp.int32, (width, width), 0)
    col = lax.broadcasted_iota(jnp.int32, (width, width), 1)
    parity = row & col & (half - 1)
    parity = parity ^ (parity >> 4)
    parity = parity ^ (parity >> 2)
    parity = (parity ^ (parity >> 1)) & 1
    same = (row >= half) == (col >= half)
    return jnp.where(same, (1 - 2 * parity).astype(jnp.float32), 0.0).astype(jnp.bfloat16)


def codes_of(rows_ref, scale_of, signs, rot_scr):
    tokens, heads, width = rows_ref.shape
    half = width // 2
    flat = rows_ref[...].reshape(tokens * heads, width)
    rotated = jnp.dot(flat, signs, preferred_element_type=jnp.float32)
    rotated = rotated * (1.0 / math.sqrt(half))
    for w in range(2):
        rot_scr[w] = rotated[:, w * half : (w + 1) * half]
    found = []
    for j in range(heads):
        parts = []
        for w in range(2):
            own = rot_scr[w, pl.ds(j, tokens, stride=heads), :] if heads > 1 else rot_scr[w]
            parts.append(jnp.clip(own / scale_of(j, w), -448.0, 448.0).astype(jnp.bfloat16))
        found.append(parts)
    return found


def page_places(slots_ref, ctx_id, tokens):
    pages = slots_ref.shape[1]
    row = lax.broadcasted_iota(jnp.int32, (tokens, pages), 0)
    page = lax.broadcasted_iota(jnp.int32, (tokens, pages), 1)
    slot = ctx_id * (tokens // BLK) + (row >> 4)
    place = (page * BLK + (row & (BLK - 1))).astype(jnp.float32)
    hit = jnp.broadcast_to(slots_ref[...], (tokens, pages)) == slot
    return jnp.sum(jnp.where(hit, place, 0.0), axis=1, keepdims=True)


def picker(distance, offset, count):
    key = lax.broadcasted_iota(jnp.int32, distance.shape, 1)
    hit = (distance == offset.astype(jnp.float32)) & (key < count)
    return jnp.where(hit, 1.0, 0.0).astype(jnp.bfloat16)


def spans_of(count_refs, info_ref, steps, tokens):
    if info_ref is not None:
        return [(info_ref[0, 0], info_ref[0, 1])]
    me = lax.axis_index("ctx")
    known = [ref[0:1, :][0, 0] for ref in count_refs]
    known.append(tokens * 3 - known[0] - known[1] - known[2])
    spans = []
    for step in steps:
        ident = me ^ step
        offset = jnp.int32(0)
        for other in range(4):
            offset = offset + jnp.where((me ^ other) < ident, known[other], 0)
        spans.append((offset, known[step]))
    return spans


def ready_kernel(*refs):
    sources, refs = refs[:6], refs[6:]
    ints_out, floats_out, signs_out, place_out, codes_out, query_ref, rot_scr = refs[:7]
    start_ref, scale_ref, count_ref, slots_ref, rows_ref, sems = refs[7:]
    held = (start_ref, scale_ref, count_ref, slots_ref, rows_ref, query_ref)
    copies = [pltpu.make_async_copy(a, b, sems.at[i]) for i, (a, b) in enumerate(zip(sources, held))]
    for copy in copies:
        copy.start()
    tokens, heads, width = rows_ref.shape
    sets, rows, _ = query_ref.shape
    ctx_id = lax.axis_index("ctx")
    rep_id = lax.axis_index("rep")
    pair_head = lax.axis_index("head") * lax.axis_size("rep") * heads
    signs = sign_pair(width)
    signs_out[...] = signs
    ints_out[...] = jnp.zeros(ints_out.shape, jnp.int32)
    floats_out[...] = jnp.zeros(floats_out.shape, jnp.float32)
    for copy in copies[:5]:
        copy.wait()
    ints_out[0:1, :] = jnp.full((1, 128), count_ref[0], jnp.int32)
    for c in range(sets):
        ints_out[1 + c : 2 + c, :] = jnp.full((1, 128), start_ref[c] + ctx_id * rows, jnp.int32)
    for side, member in enumerate((rep_id, 1 - rep_id)):
        for j in range(heads):
            for w in range(2):
                scale = scale_ref[w, pair_head + member * heads + j]
                at = (side * heads + j) * 2 + w
                floats_out[at : at + 1, :] = jnp.full((1, 128), scale, jnp.float32)
    place = jnp.broadcast_to(page_places(slots_ref, ctx_id, tokens), (tokens, tokens))
    token = lax.broadcasted_iota(jnp.int32, (tokens, tokens), 1)
    place_out[...] = place - token.astype(jnp.float32)
    found = codes_of(rows_ref, scale_reader(floats_out, 0, heads), signs, rot_scr)
    codes_out[...] = jnp.concatenate([part for parts in found for part in parts], axis=1)
    copies[5].wait()


def scale_reader(floats_ref, side, heads):
    def scale_of(j, w):
        at = (side * heads + j) * 2 + w
        return floats_ref[at : at + 1, :]

    return scale_of


def make_ready(starts, scales, counts, slots, rows, query):
    tokens, heads, width = rows.shape
    half = width // 2
    return pl.pallas_call(
        ready_kernel,
        out_shape=[
            jax.ShapeDtypeStruct((8, 128), jnp.int32),
            jax.ShapeDtypeStruct((8, 128), jnp.float32),
            jax.ShapeDtypeStruct((width, width), jnp.bfloat16),
            jax.ShapeDtypeStruct((tokens, tokens), jnp.float32),
            jax.ShapeDtypeStruct((tokens, heads * width), jnp.bfloat16),
            jax.ShapeDtypeStruct(query.shape, query.dtype),
        ],
        in_specs=[pl.BlockSpec(memory_space=pltpu.HBM)] * 6,
        out_specs=[VMEM_SPEC] * 6,
        scratch_shapes=[
            pltpu.VMEM((2, tokens * heads, half), jnp.float32),
            pltpu.SMEM(starts.shape, jnp.int32),
            pltpu.SMEM(scales.shape, jnp.float32),
            pltpu.SMEM(counts.shape, jnp.int32),
            pltpu.VMEM(slots.shape, jnp.int32),
            pltpu.VMEM(rows.shape, rows.dtype),
            pltpu.SemaphoreType.DMA((6,)),
        ],
        compiler_params=pltpu.CompilerParams(vmem_limit_bytes=VMEM_LIMIT),
        cost_estimate=pl.CostEstimate(
            flops=tokens * heads * width * width * 2, bytes_accessed=2 << 20, transcendentals=0
        ),
    )(starts, scales, counts, slots, rows, query)


def attend_kernel(metas, steps, with_codes, has_state, last, with_pages, *refs):
    refs = list(refs)
    info_ref = refs.pop(0) if metas == 0 else None
    count_refs = [refs.pop(0) for _ in range(metas)]
    ints_ref, floats_ref, signs_ref, query_ref = [refs.pop(0) for _ in range(4)]
    codes_ref = refs.pop(0) if with_codes else None
    rows_refs = [refs.pop(0) for _ in range(len(steps) - with_codes)]
    state = [refs.pop(0) for _ in range(2)] if has_state else None
    place_ref = refs.pop(0) if with_pages else None
    out_ref = refs.pop(0)
    level_out = None if last else refs.pop(0)
    moved_out = refs.pop(0) if with_pages else None
    rot_scr = refs.pop(0)

    tokens, heads, width = rows_refs[0].shape
    half = width // 2
    sets, rows, query_width = query_ref.shape
    group = query_width // half // heads
    stack = group * rows
    shards = len(steps)
    spans = spans_of(count_refs, info_ref, steps, tokens)
    bases = [ints_ref[1 + c : 2 + c, :][0, 0] for c in range(sets)]
    scale_of = scale_reader(floats_ref, 0, heads)

    def compute():
        signs = signs_ref[...]
        per_shard = []
        if with_codes:
            per_shard.append(
                [
                    [codes_ref[:, (2 * j + w) * half : (2 * j + w + 1) * half] for w in range(2)]
                    for j in range(heads)
                ]
            )
        per_shard += [codes_of(r, scale_of, signs, rot_scr) for r in rows_refs]

        def joined(j, w):
            parts = [found[j][w] for found in per_shard]
            return jnp.concatenate(parts, axis=0) if shards > 1 else parts[0]

        keys = [joined(j, 0) for j in range(heads)]
        ones = jnp.ones((shards * tokens, half), jnp.bfloat16)
        values = [jnp.concatenate([joined(j, 1), ones], axis=1) for j in range(heads)]
        row = lax.broadcasted_iota(jnp.int32, (rows, tokens), 0)
        key = lax.broadcasted_iota(jnp.int32, (rows, tokens), 1)
        for c in range(sets):
            parts = []
            for offset, count in spans:
                counted = (key < count) & (key + (offset - bases[c]) <= row)
                parts.append(jnp.where(counted, 0.0, MASKED))
            bias = jnp.concatenate(parts, axis=1) if shards > 1 else parts[0]
            bias = jnp.concatenate([bias] * group, axis=0)
            for j in range(heads):
                factor = scale_of(j, 0) * LOG2E
                stacked = jnp.concatenate(
                    [
                        query_ref[c, :, (j * group + g) * half : (j * group + g + 1) * half]
                        for g in range(group)
                    ],
                    axis=0,
                )
                scores = lax.dot_general(
                    stacked, keys[j], (((1,), (1,)), ((), ())), preferred_element_type=jnp.float32
                )
                scores = scores + bias
                top = jnp.max(scores, axis=1, keepdims=True)
                top = jnp.broadcast_to(top, (stack, half))
                if has_state:
                    level = state[1][c, j]
                    top = jnp.maximum(top, level)
                else:
                    top = jnp.maximum(top, FLOOR)
                probs = []
                for i in range(0, scores.shape[1], half):
                    part = scores[:, i : min(i + half, scores.shape[1])]
                    size = part.shape[1]
                    part = jnp.exp2((part - top[:, :size]) * factor[:, :size])
                    probs.append(part.astype(jnp.bfloat16))
                weighted = jnp.dot(
                    jnp.concatenate(probs, axis=1), values[j], preferred_element_type=jnp.float32
                )
                acc = weighted[:, :half] * scale_of(j, 1)
                total = weighted[:, half:]
                if has_state:
                    alpha = jnp.exp2((level - top) * factor)
                    total = total + alpha
                else:
                    total = jnp.maximum(total, TINY)
                for g in range(group):
                    one = slice(g * rows, (g + 1) * rows)
                    cols = slice((j * group + g) * half, (j * group + g + 1) * half)
                    part = acc[one]
                    if has_state:
                        part = part + state[0][c, :, cols].astype(jnp.float32) * alpha[one]
                    out_ref[c, :, cols] = (part / total[one]).astype(jnp.bfloat16)
                if not last:
                    level_out[c, j] = top + jnp.log2(total) / factor
        return per_shard

    if last:
        latest = bases[0]
        for base in bases[1:]:
            latest = jnp.maximum(latest, base)
        needed = spans[0][0] < latest + rows

        @pl.when(needed)
        def _():
            compute()

        @pl.when(jnp.logical_not(needed))
        def _():
            out_ref[...] = state[0][...]

    else:
        per_shard = compute()
    if with_pages:
        place = place_ref[...]
        total = None
        for (offset, count), found in zip(spans, per_shard):
            pick = picker(place, offset, count)
            own = jnp.concatenate([part for parts in found for part in parts], axis=1)
            part = jnp.dot(pick, own, preferred_element_type=jnp.float32)
            total = part if total is None else total + part
        moved_out[...] = total.astype(jnp.bfloat16)


def attend(counts, info, steps, ready, rows, codes=None, state=None, last=False):
    ints, floats, signs, place, _, query = ready
    tokens, heads, width = rows[0].shape
    half = width // 2
    sets, query_rows, query_width = query.shape
    group = query_width // half // heads
    args = list(counts) if info is None else [info]
    specs = [VMEM_SPEC] * len(counts) if info is None else [SMEM_SPEC]
    args += [ints, floats, signs, query]
    if codes is not None:
        args.append(codes)
    args += rows
    if state is not None:
        args += list(state)
    if not last:
        args.append(place)
    specs += [VMEM_SPEC] * (len(args) - len(specs))
    outs = [jax.ShapeDtypeStruct(query.shape, jnp.bfloat16)]
    out_specs = [VMEM_SPEC]
    scratch = [pltpu.VMEM((2, tokens * heads, half), jnp.float32)]
    if not last:
        outs += [
            jax.ShapeDtypeStruct((sets, heads, group * query_rows, half), jnp.float32),
            jax.ShapeDtypeStruct((tokens, heads * width), jnp.bfloat16),
        ]
        out_specs += [VMEM_SPEC] * 2
    keys = tokens * len(steps)
    work = sets * heads * group * query_rows * keys
    return pl.pallas_call(
        functools.partial(
            attend_kernel,
            len(counts) if info is None else 0,
            steps,
            codes is not None,
            state is not None,
            last,
            not last,
        ),
        out_shape=outs,
        in_specs=specs,
        out_specs=out_specs,
        scratch_shapes=scratch,
        compiler_params=pltpu.CompilerParams(vmem_limit_bytes=VMEM_LIMIT),
        cost_estimate=pl.CostEstimate(
            flops=work * half * 8, bytes_accessed=4 << 20, transcendentals=work
        ),
    )(*args)


def finish_kernel(metas, steps, *refs):
    refs = list(refs)
    info_ref = refs.pop(0) if metas == 0 else None
    count_refs = [refs.pop(0) for _ in range(metas)]
    floats_ref, signs_ref, place_ref, result_ref, own, other, own_rows, other_rows = refs[:8]
    attention_out, cache_out, rot_scr, cache_scr, sems = refs[8:]
    tokens, heads, width = own_rows.shape
    half = width // 2
    sets = result_ref.shape[0]
    rep_id = lax.axis_index("rep")
    sent = [
        pltpu.make_async_copy(result_ref.at[c], attention_out.at[c], sems.at[c]) for c in range(sets)
    ]
    for copy in sent:
        copy.start()
    signs = signs_ref[...]
    ((offset, count),) = spans_of(count_refs, info_ref, steps, tokens)
    pick = picker(place_ref[...], offset, count)
    sides = []
    for side, (moved, rows) in enumerate(((own, own_rows), (other, other_rows))):
        scale_of = scale_reader(floats_ref, side, heads)
        sides.append((moved, scale_of, codes_of(rows, scale_of, signs, rot_scr)))
    size = tokens // PIECES
    pieces = [
        pltpu.make_async_copy(
            cache_scr.at[pl.ds(i * size, size)],
            cache_out.at[pl.ds(i * size, size)],
            sems.at[sets + i],
        )
        for i in range(PIECES)
    ]

    for turn in range(2):

        @pl.when(rep_id == turn)
        def _(turn=turn):
            for i, piece in enumerate(pieces):
                here = slice(i * size, (i + 1) * size)
                for side, (moved, scale_of, found) in enumerate(sides):
                    first = (side if turn == 0 else 1 - side) * heads
                    for j in range(heads):
                        for w in range(2):
                            cols = slice((2 * j + w) * half, (2 * j + w + 1) * half)
                            part = jnp.dot(
                                pick[here], found[j][w], preferred_element_type=jnp.float32
                            )
                            part = (part + moved[here, cols].astype(jnp.float32)) * scale_of(j, w)
                            cache_scr[here, first + j, w * half : (w + 1) * half] = part
                piece.start()

    for copy in sent + pieces:
        copy.wait()


def finish(counts, info, steps, ready, result, own, other, own_rows, other_rows):
    _, floats, signs, place, _, _ = ready
    tokens, heads, width = own_rows.shape
    cache = (tokens, 2 * heads, width)
    args = list(counts) if info is None else [info]
    specs = [VMEM_SPEC] * len(counts) if info is None else [SMEM_SPEC]
    args += [floats, signs, place, result, own, other, own_rows, other_rows]
    specs += [VMEM_SPEC] * 8
    return pl.pallas_call(
        functools.partial(finish_kernel, len(counts) if info is None else 0, steps),
        out_shape=[
            jax.ShapeDtypeStruct(result.shape, result.dtype),
            jax.ShapeDtypeStruct(cache, jnp.float32),
        ],
        in_specs=specs,
        out_specs=[pl.BlockSpec(memory_space=pl.ANY)] * 2,
        scratch_shapes=[
            pltpu.VMEM((2, tokens * heads, width // 2), jnp.float32),
            pltpu.VMEM(cache, jnp.float32),
            pltpu.SemaphoreType.DMA((result.shape[0] + PIECES,)),
        ],
        compiler_params=pltpu.CompilerParams(vmem_limit_bytes=VMEM_LIMIT),
        cost_estimate=pl.CostEstimate(
            flops=tokens * tokens * heads * width * 8, bytes_accessed=2 << 20, transcendentals=0
        ),
    )(*args)


def pair(value, axis, step):
    size = lax.axis_size(axis)
    return lax.ppermute(value, axis, [(i, i ^ step) for i in range(size)])


def body(kv_rows, kv_scales, queries, shard_counts, span_starts, block_slots):
    across = pair(kv_rows, "ctx", 2)
    beside = pair(kv_rows, "ctx", 1)
    ready = make_ready(
        span_starts, kv_scales.T, shard_counts, block_slots[None, :], kv_rows, queries
    )
    count = jnp.broadcast_to(shard_counts[:, None], (8, 128))
    counts = [count, pair(count, "ctx", 1), pair(count, "ctx", 2)]
    corner = pair(across, "ctx", 1)
    *state, moved = attend(counts, None, (0, 1, 2), ready, [beside, across], ready[4])
    moved_other = pair(moved, "rep", 1)
    corner_other = pair(corner, "rep", 1)
    (result,) = attend(counts, None, (3,), ready, [corner], None, state, True)
    return finish(counts, None, (3,), ready, result, moved, moved_other, corner, corner_other)


def body_any(kv_rows, kv_scales, queries, shard_counts, span_starts, block_slots):
    counts = lax.all_gather(shard_counts, "ctx", axis=0, tiled=True)
    info = jnp.stack([jnp.cumsum(counts) - counts, counts], axis=1)
    every = lax.all_gather(kv_rows, "ctx", axis=0)
    ready = make_ready(
        span_starts, kv_scales.T, shard_counts, block_slots[None, :], kv_rows, queries
    )

    def step(carry, turn):
        state, moved = carry
        rows, one = turn
        *state, found = attend([], one[None], (0,), ready, [rows], None, state)
        return (tuple(state), moved + found), None

    *state, moved = attend([], info[:1], (0,), ready, [every[0]])
    (state, moved), _ = lax.scan(step, (tuple(state), moved), (every[1:], info[1:]))
    none = jnp.zeros((1, 2), jnp.int32)
    other = pair(moved, "rep", 1)
    return finish([], none, (0,), ready, state[0], moved, other, kv_rows, kv_rows)


def solution(mesh):
    in_specs = (
        P(("groups", "ctx"), ("head", "rep"), None),
        P(),
        P(None, ("groups", "ctx"), ("head", "rep")),
        P(("groups", "ctx")),
        P("groups"),
        P("groups"),
    )
    out_specs = (P(None, ("groups", "ctx"), ("head", "rep")), P(("groups", "ctx"), "head", None))
    chosen = body if mesh.shape["ctx"] == 4 else body_any
    return jax.shard_map(chosen, mesh=mesh, in_specs=in_specs, out_specs=out_specs, check_vma=False)
```

```python
import functools
import math

import jax
import jax.numpy as jnp
from jax import lax
from jax.experimental import pallas as pl
from jax.experimental.pallas import tpu as pltpu
from jax.sharding import PartitionSpec as P

BLK = 16
FLOOR = -1e9
MASKED = -1e30
TINY = 1e-30
FAR = 60.0
PIECES = 4
LOG2E = math.log2(math.e)
VMEM_LIMIT = 48 * 1024 * 1024
SMEM_SPEC = pl.BlockSpec(memory_space=pltpu.SMEM)
VMEM_SPEC = pl.BlockSpec(memory_space=pltpu.VMEM)


def sign_pair(width):
    half = width // 2
    row = lax.broadcasted_iota(jnp.int32, (width, width), 0)
    col = lax.broadcasted_iota(jnp.int32, (width, width), 1)
    parity = row & col & (half - 1)
    parity = parity ^ (parity >> 4)
    parity = parity ^ (parity >> 2)
    parity = (parity ^ (parity >> 1)) & 1
    same = (row >= half) == (col >= half)
    return jnp.where(same, (1 - 2 * parity).astype(jnp.float32), 0.0).astype(jnp.bfloat16)


def codes_of(rows_ref, scale_of, signs, rot_scr):
    tokens, heads, width = rows_ref.shape
    half = width // 2
    flat = rows_ref[...].reshape(tokens * heads, width)
    rotated = jnp.dot(flat, signs, preferred_element_type=jnp.float32)
    rotated = rotated * (1.0 / math.sqrt(half))
    for w in range(2):
        rot_scr[w] = rotated[:, w * half : (w + 1) * half]
    found = []
    for j in range(heads):
        parts = []
        for w in range(2):
            own = rot_scr[w, pl.ds(j, tokens, stride=heads), :] if heads > 1 else rot_scr[w]
            parts.append(jnp.clip(own / scale_of(j, w), -448.0, 448.0).astype(jnp.bfloat16))
        found.append(parts)
    return found


def page_places(slots_ref, ctx_id, tokens):
    pages = slots_ref.shape[1]
    row = lax.broadcasted_iota(jnp.int32, (tokens, pages), 0)
    page = lax.broadcasted_iota(jnp.int32, (tokens, pages), 1)
    slot = ctx_id * (tokens // BLK) + (row >> 4)
    place = (page * BLK + (row & (BLK - 1))).astype(jnp.float32)
    hit = jnp.broadcast_to(slots_ref[...], (tokens, pages)) == slot
    return jnp.sum(jnp.where(hit, place, 0.0), axis=1, keepdims=True)


def picker(distance, offset, count):
    key = lax.broadcasted_iota(jnp.int32, distance.shape, 1)
    hit = (distance == offset.astype(jnp.float32)) & (key < count)
    return jnp.where(hit, 1.0, 0.0).astype(jnp.bfloat16)


def spans_of(count_refs, info_ref, steps, tokens):
    if info_ref is not None:
        return [(info_ref[0, 0], info_ref[0, 1])]
    me = lax.axis_index("ctx")
    known = [ref[0:1, :][0, 0] for ref in count_refs]
    known.append(tokens * 3 - known[0] - known[1] - known[2])
    spans = []
    for step in steps:
        ident = me ^ step
        offset = jnp.int32(0)
        for other in range(4):
            offset = offset + jnp.where((me ^ other) < ident, known[other], 0)
        spans.append((offset, known[step]))
    return spans


def ready_kernel(*refs):
    sources, refs = refs[:6], refs[6:]
    ints_out, floats_out, signs_out, place_out, codes_out, query_ref, rot_scr = refs[:7]
    start_ref, scale_ref, count_ref, slots_ref, rows_ref, sems = refs[7:]
    held = (start_ref, scale_ref, count_ref, slots_ref, rows_ref, query_ref)
    copies = [pltpu.make_async_copy(a, b, sems.at[i]) for i, (a, b) in enumerate(zip(sources, held))]
    for copy in copies:
        copy.start()
    tokens, heads, width = rows_ref.shape
    sets, rows, _ = query_ref.shape
    ctx_id = lax.axis_index("ctx")
    rep_id = lax.axis_index("rep")
    pair_head = lax.axis_index("head") * lax.axis_size("rep") * heads
    signs = sign_pair(width)
    signs_out[...] = signs
    ints_out[...] = jnp.zeros(ints_out.shape, jnp.int32)
    floats_out[...] = jnp.zeros(floats_out.shape, jnp.float32)
    for copy in copies[:5]:
        copy.wait()
    ints_out[0:1, :] = jnp.full((1, 128), count_ref[0], jnp.int32)
    for c in range(sets):
        ints_out[1 + c : 2 + c, :] = jnp.full((1, 128), start_ref[c] + ctx_id * rows, jnp.int32)
    for side, member in enumerate((rep_id, 1 - rep_id)):
        for j in range(heads):
            for w in range(2):
                scale = scale_ref[w, pair_head + member * heads + j]
                at = (side * heads + j) * 2 + w
                floats_out[at : at + 1, :] = jnp.full((1, 128), scale, jnp.float32)
    place = jnp.broadcast_to(page_places(slots_ref, ctx_id, tokens), (tokens, tokens))
    token = lax.broadcasted_iota(jnp.int32, (tokens, tokens), 1)
    place_out[...] = place - token.astype(jnp.float32)
    found = codes_of(rows_ref, scale_reader(floats_out, 0, heads), signs, rot_scr)
    codes_out[...] = jnp.concatenate([part for parts in found for part in parts], axis=1)
    copies[5].wait()


def scale_reader(floats_ref, side, heads):
    def scale_of(j, w):
        at = (side * heads + j) * 2 + w
        return floats_ref[at : at + 1, :]

    return scale_of


def make_ready(starts, scales, counts, slots, rows, query):
    tokens, heads, width = rows.shape
    half = width // 2
    return pl.pallas_call(
        ready_kernel,
        out_shape=[
            jax.ShapeDtypeStruct((8, 128), jnp.int32),
            jax.ShapeDtypeStruct((8, 128), jnp.float32),
            jax.ShapeDtypeStruct((width, width), jnp.bfloat16),
            jax.ShapeDtypeStruct((tokens, tokens), jnp.float32),
            jax.ShapeDtypeStruct((tokens, heads * width), jnp.bfloat16),
            jax.ShapeDtypeStruct(query.shape, query.dtype),
        ],
        in_specs=[pl.BlockSpec(memory_space=pltpu.HBM)] * 6,
        out_specs=[VMEM_SPEC] * 6,
        scratch_shapes=[
            pltpu.VMEM((2, tokens * heads, half), jnp.float32),
            pltpu.SMEM(starts.shape, jnp.int32),
            pltpu.SMEM(scales.shape, jnp.float32),
            pltpu.SMEM(counts.shape, jnp.int32),
            pltpu.VMEM(slots.shape, jnp.int32),
            pltpu.VMEM(rows.shape, rows.dtype),
            pltpu.SemaphoreType.DMA((6,)),
        ],
        compiler_params=pltpu.CompilerParams(vmem_limit_bytes=VMEM_LIMIT),
        cost_estimate=pl.CostEstimate(
            flops=tokens * heads * width * width * 2, bytes_accessed=2 << 20, transcendentals=0
        ),
    )(starts, scales, counts, slots, rows, query)


def attend_kernel(metas, steps, with_codes, has_state, last, with_pages, *refs):
    refs = list(refs)
    info_ref = refs.pop(0) if metas == 0 else None
    count_refs = [refs.pop(0) for _ in range(metas)]
    ints_ref, floats_ref, signs_ref, query_ref = [refs.pop(0) for _ in range(4)]
    codes_ref = refs.pop(0) if with_codes else None
    rows_refs = [refs.pop(0) for _ in range(len(steps) - with_codes)]
    state = [refs.pop(0) for _ in range(2)] if has_state else None
    place_ref = refs.pop(0) if with_pages else None
    out_ref = refs.pop(0)
    level_out = None if last else refs.pop(0)
    moved_out = refs.pop(0) if with_pages else None
    rot_scr = refs.pop(0)

    tokens, heads, width = rows_refs[0].shape
    half = width // 2
    sets, rows, query_width = query_ref.shape
    group = query_width // half // heads
    stack = group * rows
    shards = len(steps)
    spans = spans_of(count_refs, info_ref, steps, tokens)
    bases = [ints_ref[1 + c : 2 + c, :][0, 0] for c in range(sets)]
    scale_of = scale_reader(floats_ref, 0, heads)

    def operands():
        signs = signs_ref[...]
        per_shard = []
        if with_codes:
            per_shard.append(
                [
                    [codes_ref[:, (2 * j + w) * half : (2 * j + w + 1) * half] for w in range(2)]
                    for j in range(heads)
                ]
            )
        per_shard += [codes_of(r, scale_of, signs, rot_scr) for r in rows_refs]

        def joined(j, w):
            parts = [found[j][w] for found in per_shard]
            return jnp.concatenate(parts, axis=0) if shards > 1 else parts[0]

        keys = [joined(j, 0) for j in range(heads)]
        ones = jnp.ones((shards * tokens, half), jnp.bfloat16)
        values = [jnp.concatenate([joined(j, 1), ones], axis=1) for j in range(heads)]
        row = lax.broadcasted_iota(jnp.int32, (rows, tokens), 0)
        key = lax.broadcasted_iota(jnp.int32, (rows, tokens), 1)
        biases = []
        for c in range(sets):
            parts = []
            for offset, count in spans:
                counted = (key < count) & (key + (offset - bases[c]) <= row)
                parts.append(jnp.where(counted, 0.0, MASKED))
            bias = jnp.concatenate(parts, axis=1) if shards > 1 else parts[0]
            biases.append(jnp.concatenate([bias] * group, axis=0))
        return per_shard, keys, values, biases

    def scores_of(c, j, keys, biases):
        stacked = jnp.concatenate(
            [
                query_ref[c, :, (j * group + g) * half : (j * group + g + 1) * half]
                for g in range(group)
            ],
            axis=0,
        )
        scores = lax.dot_general(
            stacked, keys[j], (((1,), (1,)), ((), ())), preferred_element_type=jnp.float32
        )
        return scores + biases[c]

    def tiles(scores):
        for i in range(0, scores.shape[1], half):
            yield scores[:, i : min(i + half, scores.shape[1])]

    def compute_near():
        _, keys, values, biases = operands()
        worst = jnp.full((8, half), FLOOR, jnp.float32)
        for c in range(sets):
            for j in range(heads):
                factor = scale_of(j, 0) * LOG2E
                level = state[1][c, j]
                probs = []
                for part in tiles(scores_of(c, j, keys, biases)):
                    size = part.shape[1]
                    part = (part - level[:, :size]) * factor[:, :size]
                    high = jnp.max(part.reshape(stack // 8, 8, size), axis=0)
                    if size < half:
                        high = jnp.concatenate([high, worst[:, size:]], axis=1)
                    worst = jnp.maximum(worst, high)
                    probs.append(jnp.exp2(part).astype(jnp.bfloat16))
                weighted = jnp.dot(
                    jnp.concatenate(probs, axis=1), values[j], preferred_element_type=jnp.float32
                )
                share = 1.0 / (weighted[:, half:] + 1.0)
                for g in range(group):
                    one = slice(g * rows, (g + 1) * rows)
                    cols = slice((j * group + g) * half, (j * group + g + 1) * half)
                    part = weighted[one, :half] * scale_of(j, 1)
                    part = (part + state[0][c, :, cols].astype(jnp.float32)) * share[one]
                    out_ref[c, :, cols] = part.astype(jnp.bfloat16)
        return jnp.max(worst)

    def compute():
        per_shard, keys, values, biases = operands()
        for c in range(sets):
            for j in range(heads):
                factor = scale_of(j, 0) * LOG2E
                scores = scores_of(c, j, keys, biases)
                top = jnp.max(scores, axis=1, keepdims=True)
                top = jnp.broadcast_to(top, (stack, half))
                if has_state:
                    level = state[1][c, j]
                    top = jnp.maximum(top, level)
                else:
                    top = jnp.maximum(top, FLOOR)
                probs = []
                for part in tiles(scores):
                    size = part.shape[1]
                    part = jnp.exp2((part - top[:, :size]) * factor[:, :size])
                    probs.append(part.astype(jnp.bfloat16))
                weighted = jnp.dot(
                    jnp.concatenate(probs, axis=1), values[j], preferred_element_type=jnp.float32
                )
                acc = weighted[:, :half] * scale_of(j, 1)
                total = weighted[:, half:]
                if has_state:
                    alpha = jnp.exp2((level - top) * factor)
                    total = total + alpha
                else:
                    total = jnp.maximum(total, TINY)
                for g in range(group):
                    one = slice(g * rows, (g + 1) * rows)
                    cols = slice((j * group + g) * half, (j * group + g + 1) * half)
                    part = acc[one]
                    if has_state:
                        part = part + state[0][c, :, cols].astype(jnp.float32) * alpha[one]
                    out_ref[c, :, cols] = (part / total[one]).astype(jnp.bfloat16)
                if not last:
                    level_out[c, j] = top + jnp.log2(total) / factor
        return per_shard

    if last:
        latest = bases[0]
        for base in bases[1:]:
            latest = jnp.maximum(latest, base)
        needed = spans[0][0] < latest + rows

        @pl.when(needed)
        def _():
            worst = compute_near()

            @pl.when(worst > FAR)
            def _():
                compute()

        @pl.when(jnp.logical_not(needed))
        def _():
            out_ref[...] = state[0][...]

    else:
        per_shard = compute()
    if with_pages:
        place = place_ref[...]
        total = None
        for (offset, count), found in zip(spans, per_shard):
            pick = picker(place, offset, count)
            own = jnp.concatenate([part for parts in found for part in parts], axis=1)
            part = jnp.dot(pick, own, preferred_element_type=jnp.float32)
            total = part if total is None else total + part
        moved_out[...] = total.astype(jnp.bfloat16)


def attend(counts, info, steps, ready, rows, codes=None, state=None, last=False):
    ints, floats, signs, place, _, query = ready
    tokens, heads, width = rows[0].shape
    half = width // 2
    sets, query_rows, query_width = query.shape
    group = query_width // half // heads
    args = list(counts) if info is None else [info]
    specs = [VMEM_SPEC] * len(counts) if info is None else [SMEM_SPEC]
    args += [ints, floats, signs, query]
    if codes is not None:
        args.append(codes)
    args += rows
    if state is not None:
        args += list(state)
    if not last:
        args.append(place)
    specs += [VMEM_SPEC] * (len(args) - len(specs))
    outs = [jax.ShapeDtypeStruct(query.shape, jnp.bfloat16)]
    out_specs = [VMEM_SPEC]
    scratch = [pltpu.VMEM((2, tokens * heads, half), jnp.float32)]
    if not last:
        outs += [
            jax.ShapeDtypeStruct((sets, heads, group * query_rows, half), jnp.float32),
            jax.ShapeDtypeStruct((tokens, heads * width), jnp.bfloat16),
        ]
        out_specs += [VMEM_SPEC] * 2
    keys = tokens * len(steps)
    work = sets * heads * group * query_rows * keys
    return pl.pallas_call(
        functools.partial(
            attend_kernel,
            len(counts) if info is None else 0,
            steps,
            codes is not None,
            state is not None,
            last,
            not last,
        ),
        out_shape=outs,
        in_specs=specs,
        out_specs=out_specs,
        scratch_shapes=scratch,
        compiler_params=pltpu.CompilerParams(vmem_limit_bytes=VMEM_LIMIT),
        cost_estimate=pl.CostEstimate(
            flops=work * half * 8, bytes_accessed=4 << 20, transcendentals=work
        ),
    )(*args)


def finish_kernel(metas, steps, *refs):
    refs = list(refs)
    info_ref = refs.pop(0) if metas == 0 else None
    count_refs = [refs.pop(0) for _ in range(metas)]
    floats_ref, signs_ref, place_ref, result_ref, own, other, own_rows, other_rows = refs[:8]
    attention_out, cache_out, rot_scr, cache_scr, sems = refs[8:]
    tokens, heads, width = own_rows.shape
    half = width // 2
    sets = result_ref.shape[0]
    rep_id = lax.axis_index("rep")
    sent = [
        pltpu.make_async_copy(result_ref.at[c], attention_out.at[c], sems.at[c]) for c in range(sets)
    ]
    for copy in sent:
        copy.start()
    signs = signs_ref[...]
    ((offset, count),) = spans_of(count_refs, info_ref, steps, tokens)
    pick = picker(place_ref[...], offset, count)
    sides = []
    for side, (moved, rows) in enumerate(((own, own_rows), (other, other_rows))):
        scale_of = scale_reader(floats_ref, side, heads)
        sides.append((moved, scale_of, codes_of(rows, scale_of, signs, rot_scr)))
    size = tokens // PIECES
    pieces = [
        pltpu.make_async_copy(
            cache_scr.at[pl.ds(i * size, size)],
            cache_out.at[pl.ds(i * size, size)],
            sems.at[sets + i],
        )
        for i in range(PIECES)
    ]

    for turn in range(2):

        @pl.when(rep_id == turn)
        def _(turn=turn):
            for i, piece in enumerate(pieces):
                here = slice(i * size, (i + 1) * size)
                for side, (moved, scale_of, found) in enumerate(sides):
                    first = (side if turn == 0 else 1 - side) * heads
                    for j in range(heads):
                        for w in range(2):
                            cols = slice((2 * j + w) * half, (2 * j + w + 1) * half)
                            part = jnp.dot(
                                pick[here], found[j][w], preferred_element_type=jnp.float32
                            )
                            part = (part + moved[here, cols].astype(jnp.float32)) * scale_of(j, w)
                            cache_scr[here, first + j, w * half : (w + 1) * half] = part
                piece.start()

    for copy in sent + pieces:
        copy.wait()


def finish(counts, info, steps, ready, result, own, other, own_rows, other_rows):
    _, floats, signs, place, _, _ = ready
    tokens, heads, width = own_rows.shape
    cache = (tokens, 2 * heads, width)
    args = list(counts) if info is None else [info]
    specs = [VMEM_SPEC] * len(counts) if info is None else [SMEM_SPEC]
    args += [floats, signs, place, result, own, other, own_rows, other_rows]
    specs += [VMEM_SPEC] * 8
    return pl.pallas_call(
        functools.partial(finish_kernel, len(counts) if info is None else 0, steps),
        out_shape=[
            jax.ShapeDtypeStruct(result.shape, result.dtype),
            jax.ShapeDtypeStruct(cache, jnp.float32),
        ],
        in_specs=specs,
        out_specs=[pl.BlockSpec(memory_space=pl.ANY)] * 2,
        scratch_shapes=[
            pltpu.VMEM((2, tokens * heads, width // 2), jnp.float32),
            pltpu.VMEM(cache, jnp.float32),
            pltpu.SemaphoreType.DMA((result.shape[0] + PIECES,)),
        ],
        compiler_params=pltpu.CompilerParams(vmem_limit_bytes=VMEM_LIMIT),
        cost_estimate=pl.CostEstimate(
            flops=tokens * tokens * heads * width * 8, bytes_accessed=2 << 20, transcendentals=0
        ),
    )(*args)


def pair(value, axis, step):
    size = lax.axis_size(axis)
    return lax.ppermute(value, axis, [(i, i ^ step) for i in range(size)])


def body(kv_rows, kv_scales, queries, shard_counts, span_starts, block_slots):
    across = pair(kv_rows, "ctx", 2)
    beside = pair(kv_rows, "ctx", 1)
    ready = make_ready(
        span_starts, kv_scales.T, shard_counts, block_slots[None, :], kv_rows, queries
    )
    count = jnp.broadcast_to(shard_counts[:, None], (8, 128))
    counts = [count, pair(count, "ctx", 1), pair(count, "ctx", 2)]
    corner = pair(across, "ctx", 1)
    *state, moved = attend(counts, None, (0, 1, 2), ready, [beside, across], ready[4])
    moved_other = pair(moved, "rep", 1)
    corner_other = pair(corner, "rep", 1)
    (result,) = attend(counts, None, (3,), ready, [corner], None, state, True)
    return finish(counts, None, (3,), ready, result, moved, moved_other, corner, corner_other)


def body_any(kv_rows, kv_scales, queries, shard_counts, span_starts, block_slots):
    counts = lax.all_gather(shard_counts, "ctx", axis=0, tiled=True)
    info = jnp.stack([jnp.cumsum(counts) - counts, counts], axis=1)
    every = lax.all_gather(kv_rows, "ctx", axis=0)
    ready = make_ready(
        span_starts, kv_scales.T, shard_counts, block_slots[None, :], kv_rows, queries
    )

    def step(carry, turn):
        state, moved = carry
        rows, one = turn
        *state, found = attend([], one[None], (0,), ready, [rows], None, state)
        return (tuple(state), moved + found), None

    *state, moved = attend([], info[:1], (0,), ready, [every[0]])
    (state, moved), _ = lax.scan(step, (tuple(state), moved), (every[1:], info[1:]))
    none = jnp.zeros((1, 2), jnp.int32)
    other = pair(moved, "rep", 1)
    return finish([], none, (0,), ready, state[0], moved, other, kv_rows, kv_rows)


def solution(mesh):
    in_specs = (
        P(("groups", "ctx"), ("head", "rep"), None),
        P(),
        P(None, ("groups", "ctx"), ("head", "rep")),
        P(("groups", "ctx")),
        P("groups"),
        P("groups"),
    )
    out_specs = (P(None, ("groups", "ctx"), ("head", "rep")), P(("groups", "ctx"), "head", None))
    chosen = body if mesh.shape["ctx"] == 4 else body_any
    return jax.shard_map(chosen, mesh=mesh, in_specs=in_specs, out_specs=out_specs, check_vma=False)
```

```python
import functools
import math

import jax
import jax.numpy as jnp
from jax import lax
from jax.experimental import pallas as pl
from jax.experimental.pallas import tpu as pltpu
from jax.sharding import PartitionSpec as P

BLK = 16
FLOOR = -1e9
MASKED = -1e30
TINY = 1e-30
FAR = 2.0**60
PIECES = (6, 4, 2)
LOG2E = math.log2(math.e)
VMEM_LIMIT = 48 * 1024 * 1024
SMEM_SPEC = pl.BlockSpec(memory_space=pltpu.SMEM)
VMEM_SPEC = pl.BlockSpec(memory_space=pltpu.VMEM)


def sign_pair(width):
    half = width // 2
    row = lax.broadcasted_iota(jnp.int32, (width, width), 0)
    col = lax.broadcasted_iota(jnp.int32, (width, width), 1)
    parity = row & col & (half - 1)
    parity = parity ^ (parity >> 4)
    parity = parity ^ (parity >> 2)
    parity = (parity ^ (parity >> 1)) & 1
    same = (row >= half) == (col >= half)
    return jnp.where(same, (1 - 2 * parity).astype(jnp.float32), 0.0).astype(jnp.bfloat16)


def codes_of(rows_ref, scale_of, signs, rot_scr):
    tokens, heads, width = rows_ref.shape
    half = width // 2
    flat = rows_ref[...].reshape(tokens * heads, width)
    rotated = jnp.dot(flat, signs, preferred_element_type=jnp.float32)
    rotated = rotated * (1.0 / math.sqrt(half))
    for w in range(2):
        rot_scr[w] = rotated[:, w * half : (w + 1) * half]
    found = []
    for j in range(heads):
        parts = []
        for w in range(2):
            own = rot_scr[w, pl.ds(j, tokens, stride=heads), :] if heads > 1 else rot_scr[w]
            parts.append(jnp.clip(own / scale_of(j, w), -448.0, 448.0).astype(jnp.bfloat16))
        found.append(parts)
    return found


def page_places(slots_ref, ctx_id, tokens):
    pages = slots_ref.shape[1]
    row = lax.broadcasted_iota(jnp.int32, (tokens, pages), 0)
    page = lax.broadcasted_iota(jnp.int32, (tokens, pages), 1)
    slot = ctx_id * (tokens // BLK) + (row >> 4)
    place = (page * BLK + (row & (BLK - 1))).astype(jnp.float32)
    hit = jnp.broadcast_to(slots_ref[...], (tokens, pages)) == slot
    return jnp.sum(jnp.where(hit, place, 0.0), axis=1, keepdims=True)


def picker(distance, offset, count):
    key = lax.broadcasted_iota(jnp.int32, distance.shape, 1)
    hit = (distance == offset.astype(jnp.float32)) & (key < count)
    return jnp.where(hit, 1.0, 0.0).astype(jnp.bfloat16)


def spans_of(count_refs, info_ref, steps, tokens):
    if info_ref is not None:
        return [(info_ref[0, 0], info_ref[0, 1])]
    me = lax.axis_index("ctx")
    known = [ref[0:1, :][0, 0] for ref in count_refs]
    known.append(tokens * 3 - known[0] - known[1] - known[2])
    spans = []
    for step in steps:
        ident = me ^ step
        offset = jnp.int32(0)
        for other in range(4):
            offset = offset + jnp.where((me ^ other) < ident, known[other], 0)
        spans.append((offset, known[step]))
    return spans


def ready_kernel(*refs):
    sources, refs = refs[:6], refs[6:]
    ints_out, floats_out, signs_out, place_out, codes_out, query_ref, rot_scr = refs[:7]
    start_ref, scale_ref, count_ref, slots_ref, rows_ref, sems = refs[7:]
    held = (start_ref, scale_ref, count_ref, slots_ref, rows_ref, query_ref)
    copies = [pltpu.make_async_copy(a, b, sems.at[i]) for i, (a, b) in enumerate(zip(sources, held))]
    for copy in copies:
        copy.start()
    tokens, heads, width = rows_ref.shape
    sets, rows, _ = query_ref.shape
    ctx_id = lax.axis_index("ctx")
    rep_id = lax.axis_index("rep")
    pair_head = lax.axis_index("head") * lax.axis_size("rep") * heads
    signs = sign_pair(width)
    signs_out[...] = signs
    ints_out[...] = jnp.zeros(ints_out.shape, jnp.int32)
    floats_out[...] = jnp.zeros(floats_out.shape, jnp.float32)
    for copy in copies[:5]:
        copy.wait()
    ints_out[0:1, :] = jnp.full((1, 128), count_ref[0], jnp.int32)
    for c in range(sets):
        ints_out[1 + c : 2 + c, :] = jnp.full((1, 128), start_ref[c] + ctx_id * rows, jnp.int32)
    for side, member in enumerate((rep_id, 1 - rep_id)):
        for j in range(heads):
            for w in range(2):
                scale = scale_ref[w, pair_head + member * heads + j]
                at = (side * heads + j) * 2 + w
                floats_out[at : at + 1, :] = jnp.full((1, 128), scale, jnp.float32)
    place = jnp.broadcast_to(page_places(slots_ref, ctx_id, tokens), (tokens, tokens))
    token = lax.broadcasted_iota(jnp.int32, (tokens, tokens), 1)
    place_out[...] = place - token.astype(jnp.float32)
    found = codes_of(rows_ref, scale_reader(floats_out, 0, heads), signs, rot_scr)
    codes_out[...] = jnp.concatenate([part for parts in found for part in parts], axis=1)
    copies[5].wait()


def scale_reader(floats_ref, side, heads):
    def scale_of(j, w):
        at = (side * heads + j) * 2 + w
        return floats_ref[at : at + 1, :]

    return scale_of


def make_ready(starts, scales, counts, slots, rows, query):
    tokens, heads, width = rows.shape
    half = width // 2
    return pl.pallas_call(
        ready_kernel,
        out_shape=[
            jax.ShapeDtypeStruct((8, 128), jnp.int32),
            jax.ShapeDtypeStruct((8, 128), jnp.float32),
            jax.ShapeDtypeStruct((width, width), jnp.bfloat16),
            jax.ShapeDtypeStruct((tokens, tokens), jnp.float32),
            jax.ShapeDtypeStruct((tokens, heads * width), jnp.bfloat16),
            jax.ShapeDtypeStruct(query.shape, query.dtype),
        ],
        in_specs=[pl.BlockSpec(memory_space=pltpu.HBM)] * 6,
        out_specs=[VMEM_SPEC] * 6,
        scratch_shapes=[
            pltpu.VMEM((2, tokens * heads, half), jnp.float32),
            pltpu.SMEM(starts.shape, jnp.int32),
            pltpu.SMEM(scales.shape, jnp.float32),
            pltpu.SMEM(counts.shape, jnp.int32),
            pltpu.VMEM(slots.shape, jnp.int32),
            pltpu.VMEM(rows.shape, rows.dtype),
            pltpu.SemaphoreType.DMA((6,)),
        ],
        compiler_params=pltpu.CompilerParams(vmem_limit_bytes=VMEM_LIMIT),
        cost_estimate=pl.CostEstimate(
            flops=tokens * heads * width * width * 2, bytes_accessed=2 << 20, transcendentals=0
        ),
    )(starts, scales, counts, slots, rows, query)


def attend_kernel(metas, steps, with_codes, has_state, last, *refs):
    refs = list(refs)
    info_ref = refs.pop(0) if metas == 0 else None
    count_refs = [refs.pop(0) for _ in range(metas)]
    ints_ref, floats_ref, signs_ref, query_ref = [refs.pop(0) for _ in range(4)]
    codes_ref = refs.pop(0) if with_codes else None
    rows_refs = [refs.pop(0) for _ in range(len(steps) - with_codes)]
    state = [refs.pop(0) for _ in range(2)] if has_state else None
    place_ref = None if last else refs.pop(0)
    pick_ref, moved_ref = (refs.pop(0), refs.pop(0)) if last else (None, None)
    out_ref = refs.pop(0)
    level_out = None if last else refs.pop(0)
    moved_out = refs.pop(0)
    pick_out = refs.pop(0) if with_codes else None
    rot_scr = refs.pop(0)

    tokens, heads, width = rows_refs[0].shape
    half = width // 2
    sets, rows, query_width = query_ref.shape
    group = query_width // half // heads
    stack = group * rows
    shards = len(steps)
    spans = spans_of(count_refs, info_ref, steps, tokens)
    bases = [ints_ref[1 + c : 2 + c, :][0, 0] for c in range(sets)]
    scale_of = scale_reader(floats_ref, 0, heads)

    def shard_codes():
        per_shard = []
        if with_codes:
            per_shard.append(
                [
                    [codes_ref[:, (2 * j + w) * half : (2 * j + w + 1) * half] for w in range(2)]
                    for j in range(heads)
                ]
            )
        return per_shard + [codes_of(r, scale_of, signs_ref[...], rot_scr) for r in rows_refs]

    def operands(per_shard):
        def joined(j, w):
            parts = [found[j][w] for found in per_shard]
            return jnp.concatenate(parts, axis=0) if shards > 1 else parts[0]

        keys = [joined(j, 0) for j in range(heads)]
        ones = jnp.ones((shards * tokens, half), jnp.bfloat16)
        values = [jnp.concatenate([joined(j, 1), ones], axis=1) for j in range(heads)]
        row = lax.broadcasted_iota(jnp.int32, (tokens, half), 1)
        key = lax.broadcasted_iota(jnp.int32, (tokens, half), 0)
        masked_keys = []
        for c in range(sets):
            parts = []
            for offset, count in spans:
                counted = (key < count) & (key + (offset - bases[c]) <= row)
                parts.append(jnp.where(counted, 0.0, MASKED).astype(jnp.bfloat16))
            bias = jnp.concatenate(parts, axis=0) if shards > 1 else parts[0]
            masked_keys.append([jnp.concatenate([keys[j], bias], axis=1) for j in range(heads)])
        unit = (
            lax.broadcasted_iota(jnp.int32, (rows, half), 0)
            == lax.broadcasted_iota(jnp.int32, (rows, half), 1)
        )
        unit = jnp.where(unit, 1.0, 0.0).astype(jnp.bfloat16)
        return masked_keys, values, jnp.concatenate([unit] * group, axis=0)

    def scores_of(c, j, keys, units):
        stacked = jnp.concatenate(
            [
                query_ref[c, :, (j * group + g) * half : (j * group + g + 1) * half]
                for g in range(group)
            ],
            axis=0,
        )
        stacked = jnp.concatenate([stacked, units], axis=1)
        return lax.dot_general(
            stacked, keys[c][j], (((1,), (1,)), ((), ())), preferred_element_type=jnp.float32
        )

    def tiles(scores):
        for i in range(0, scores.shape[1], half):
            yield scores[:, i : min(i + half, scores.shape[1])]

    def compute_near(per_shard):
        keys, values, units = operands(per_shard)
        worst = jnp.zeros((8, half), jnp.float32)
        for c in range(sets):
            for j in range(heads):
                factor = scale_of(j, 0) * LOG2E
                level = state[1][c, j]
                probs = []
                for part in tiles(scores_of(c, j, keys, units)):
                    size = part.shape[1]
                    part = (part - level[:, :size]) * factor[:, :size]
                    probs.append(jnp.exp2(part).astype(jnp.bfloat16))
                weighted = jnp.dot(
                    jnp.concatenate(probs, axis=1), values[j], preferred_element_type=jnp.float32
                )
                total = weighted[:, half:]
                worst = jnp.maximum(worst, jnp.max(total.reshape(stack // 8, 8, half), axis=0))
                share = 1.0 / (total + 1.0)
                for g in range(group):
                    one = slice(g * rows, (g + 1) * rows)
                    cols = slice((j * group + g) * half, (j * group + g + 1) * half)
                    part = weighted[one, :half] * scale_of(j, 1)
                    part = (part + state[0][c, :, cols].astype(jnp.float32)) * share[one]
                    out_ref[c, :, cols] = part.astype(jnp.bfloat16)
        return jnp.max(worst)

    def compute(per_shard):
        keys, values, units = operands(per_shard)
        for c in range(sets):
            for j in range(heads):
                factor = scale_of(j, 0) * LOG2E
                scores = scores_of(c, j, keys, units)
                top = jnp.max(scores, axis=1, keepdims=True)
                top = jnp.broadcast_to(top, (stack, half))
                if has_state:
                    level = state[1][c, j]
                    top = jnp.maximum(top, level)
                else:
                    top = jnp.maximum(top, FLOOR)
                probs = []
                for part in tiles(scores):
                    size = part.shape[1]
                    part = jnp.exp2((part - top[:, :size]) * factor[:, :size])
                    probs.append(part.astype(jnp.bfloat16))
                weighted = jnp.dot(
                    jnp.concatenate(probs, axis=1), values[j], preferred_element_type=jnp.float32
                )
                acc = weighted[:, :half] * scale_of(j, 1)
                total = weighted[:, half:]
                if has_state:
                    alpha = jnp.exp2((level - top) * factor)
                    total = total + alpha
                else:
                    total = jnp.maximum(total, TINY)
                for g in range(group):
                    one = slice(g * rows, (g + 1) * rows)
                    cols = slice((j * group + g) * half, (j * group + g + 1) * half)
                    part = acc[one]
                    if has_state:
                        part = part + state[0][c, :, cols].astype(jnp.float32) * alpha[one]
                    out_ref[c, :, cols] = (part / total[one]).astype(jnp.bfloat16)
                if not last:
                    level_out[c, j] = top + jnp.log2(total) / factor

    def picked(pick, found):
        own = jnp.concatenate([part for parts in found for part in parts], axis=1)
        return jnp.dot(pick, own, preferred_element_type=jnp.float32)

    if last:

        def deliver(per_shard):
            total = picked(pick_ref[...], per_shard[0]) + moved_ref[...].astype(jnp.float32)
            moved_out[...] = total.astype(jnp.bfloat16)

        latest = bases[0]
        for base in bases[1:]:
            latest = jnp.maximum(latest, base)
        needed = spans[0][0] < latest + rows

        @pl.when(needed)
        def _():
            per_shard = shard_codes()
            worst = compute_near(per_shard)
            deliver(per_shard)

            @pl.when(worst > FAR)
            def _():
                compute(per_shard)

        @pl.when(jnp.logical_not(needed))
        def _():
            deliver(shard_codes())
            out_ref[...] = state[0][...]

    else:
        per_shard = shard_codes()
        compute(per_shard)
        place = place_ref[...]
        total = None
        for (offset, count), found in zip(spans, per_shard):
            part = picked(picker(place, offset, count), found)
            total = part if total is None else total + part
        if with_codes:
            ((offset, count),) = spans_of(count_refs, info_ref, (3,), tokens)
            pick_out[...] = picker(place, offset, count)
        moved_out[...] = total.astype(jnp.bfloat16)


def attend(counts, info, steps, ready, rows, codes=None, state=None, picked=None):
    ints, floats, signs, place, _, query = ready
    tokens, heads, width = rows[0].shape
    half = width // 2
    sets, query_rows, query_width = query.shape
    group = query_width // half // heads
    args = list(counts) if info is None else [info]
    specs = [VMEM_SPEC] * len(counts) if info is None else [SMEM_SPEC]
    args += [ints, floats, signs, query]
    if codes is not None:
        args.append(codes)
    args += rows
    if state is not None:
        args += list(state)
    last = picked is not None
    args += list(picked) if last else [place]
    specs += [VMEM_SPEC] * (len(args) - len(specs))
    outs = [jax.ShapeDtypeStruct(query.shape, jnp.bfloat16)]
    if not last:
        stacked = (sets, heads, group * query_rows, half)
        outs.append(jax.ShapeDtypeStruct(stacked, jnp.float32))
    outs.append(jax.ShapeDtypeStruct((tokens, heads * width), jnp.bfloat16))
    if codes is not None:
        outs.append(jax.ShapeDtypeStruct((tokens, tokens), jnp.bfloat16))
    keys = tokens * len(steps)
    work = sets * heads * group * query_rows * keys
    return pl.pallas_call(
        functools.partial(
            attend_kernel,
            len(counts) if info is None else 0,
            steps,
            codes is not None,
            state is not None,
            last,
        ),
        out_shape=outs,
        in_specs=specs,
        out_specs=[VMEM_SPEC] * len(outs),
        scratch_shapes=[pltpu.VMEM((2, tokens * heads, half), jnp.float32)],
        compiler_params=pltpu.CompilerParams(vmem_limit_bytes=VMEM_LIMIT),
        cost_estimate=pl.CostEstimate(
            flops=work * half * 8, bytes_accessed=4 << 20, transcendentals=work
        ),
    )(*args)


def finish_kernel(
    floats_ref, signs_ref, pick_ref, result_ref, own, other, other_rows, *outs_and_scratch
):
    attention_out, cache_out, rot_scr, cache_scr, sems = outs_and_scratch
    tokens, heads, width = other_rows.shape
    half = width // 2
    sets = result_ref.shape[0]
    rep_id = lax.axis_index("rep")
    sent = [
        pltpu.make_async_copy(result_ref.at[c], attention_out.at[c], sems.at[c]) for c in range(sets)
    ]
    for copy in sent:
        copy.start()
    scales = [scale_reader(floats_ref, side, heads) for side in range(2)]
    found = codes_of(other_rows, scales[1], signs_ref[...], rot_scr)
    pick = pick_ref[...]
    pieces = []
    start = 0
    for i, eighths in enumerate(PIECES):
        size = tokens // 12 * eighths
        here = pl.ds(start, size)
        pieces.append(
            (
                slice(start, start + size),
                pltpu.make_async_copy(cache_scr.at[here], cache_out.at[here], sems.at[sets + i]),
            )
        )
        start += size

    for turn in range(2):

        @pl.when(rep_id == turn)
        def _(turn=turn):
            for here, piece in pieces:
                for side, moved in enumerate((own, other)):
                    first = (side if turn == 0 else 1 - side) * heads
                    for j in range(heads):
                        for w in range(2):
                            cols = slice((2 * j + w) * half, (2 * j + w + 1) * half)
                            part = moved[here, cols].astype(jnp.float32)
                            if side == 1:
                                part = part + jnp.dot(
                                    pick[here], found[j][w], preferred_element_type=jnp.float32
                                )
                            part = part * scales[side](j, w)
                            cache_scr[here, first + j, w * half : (w + 1) * half] = part
                piece.start()

    for copy in sent + [piece for _, piece in pieces]:
        copy.wait()


def finish(ready, pick, result, own, other, other_rows):
    _, floats, signs, _, _, _ = ready
    tokens, heads, width = other_rows.shape
    cache = (tokens, 2 * heads, width)
    args = [floats, signs, pick, result, own, other, other_rows]
    return pl.pallas_call(
        finish_kernel,
        out_shape=[
            jax.ShapeDtypeStruct(result.shape, result.dtype),
            jax.ShapeDtypeStruct(cache, jnp.float32),
        ],
        in_specs=[VMEM_SPEC] * len(args),
        out_specs=[pl.BlockSpec(memory_space=pl.ANY)] * 2,
        scratch_shapes=[
            pltpu.VMEM((2, tokens * heads, width // 2), jnp.float32),
            pltpu.VMEM(cache, jnp.float32),
            pltpu.SemaphoreType.DMA((result.shape[0] + len(PIECES),)),
        ],
        compiler_params=pltpu.CompilerParams(vmem_limit_bytes=VMEM_LIMIT),
        cost_estimate=pl.CostEstimate(
            flops=tokens * tokens * heads * width * 4, bytes_accessed=2 << 20, transcendentals=0
        ),
    )(*args)


def pair(value, axis, step):
    size = lax.axis_size(axis)
    return lax.ppermute(value, axis, [(i, i ^ step) for i in range(size)])


def body(kv_rows, kv_scales, queries, shard_counts, span_starts, block_slots):
    across = pair(kv_rows, "ctx", 2)
    beside = pair(kv_rows, "ctx", 1)
    ready = make_ready(
        span_starts, kv_scales.T, shard_counts, block_slots[None, :], kv_rows, queries
    )
    count = jnp.broadcast_to(shard_counts[:, None], (8, 128))
    counts = [count, pair(count, "ctx", 1), pair(count, "ctx", 2)]
    corner = pair(across, "ctx", 1)
    *state, moved, pick = attend(counts, None, (0, 1, 2), ready, [beside, across], ready[4])
    moved_other = pair(moved, "rep", 1)
    corner_other = pair(corner, "rep", 1)
    result, own = attend(counts, None, (3,), ready, [corner], None, state, (pick, moved))
    return finish(ready, pick, result, own, moved_other, corner_other)


def body_any(kv_rows, kv_scales, queries, shard_counts, span_starts, block_slots):
    counts = lax.all_gather(shard_counts, "ctx", axis=0, tiled=True)
    info = jnp.stack([jnp.cumsum(counts) - counts, counts], axis=1)
    every = lax.all_gather(kv_rows, "ctx", axis=0)
    ready = make_ready(
        span_starts, kv_scales.T, shard_counts, block_slots[None, :], kv_rows, queries
    )

    def step(carry, turn):
        state, moved = carry
        rows, one = turn
        *state, found = attend([], one[None], (0,), ready, [rows], None, state)
        return (tuple(state), moved + found), None

    *state, moved = attend([], info[:1], (0,), ready, [every[0]])
    (state, moved), _ = lax.scan(step, (tuple(state), moved), (every[1:], info[1:]))
    none = jnp.zeros((kv_rows.shape[0],) * 2, jnp.bfloat16)
    return finish(ready, none, state[0], moved, pair(moved, "rep", 1), kv_rows)


def solution(mesh):
    in_specs = (
        P(("groups", "ctx"), ("head", "rep"), None),
        P(),
        P(None, ("groups", "ctx"), ("head", "rep")),
        P(("groups", "ctx")),
        P("groups"),
        P("groups"),
    )
    out_specs = (P(None, ("groups", "ctx"), ("head", "rep")), P(("groups", "ctx"), "head", None))
    chosen = body if mesh.shape["ctx"] == 4 else body_any
    return jax.shard_map(chosen, mesh=mesh, in_specs=in_specs, out_specs=out_specs, check_vma=False)
```

```python
import functools
import math

import jax
import jax.numpy as jnp
from jax import lax
from jax.experimental import pallas as pl
from jax.experimental.pallas import tpu as pltpu
from jax.sharding import PartitionSpec as P

BLK = 16
FLOOR = -1e9
MASKED = -1e30
TINY = 1e-30
FAR = 2.0**60
PIECES = (6, 4, 2)
LOG2E = math.log2(math.e)
VMEM_LIMIT = 48 * 1024 * 1024
SMEM_SPEC = pl.BlockSpec(memory_space=pltpu.SMEM)
VMEM_SPEC = pl.BlockSpec(memory_space=pltpu.VMEM)


def sign_pair(width):
    half = width // 2
    row = lax.broadcasted_iota(jnp.int32, (width, width), 0)
    col = lax.broadcasted_iota(jnp.int32, (width, width), 1)
    parity = row & col & (half - 1)
    parity = parity ^ (parity >> 4)
    parity = parity ^ (parity >> 2)
    parity = (parity ^ (parity >> 1)) & 1
    same = (row >= half) == (col >= half)
    return jnp.where(same, (1 - 2 * parity).astype(jnp.float32), 0.0).astype(jnp.bfloat16)


def codes_of(rows_ref, scale_of, signs, rot_scr):
    tokens, heads, width = rows_ref.shape
    half = width // 2
    flat = rows_ref[...].reshape(tokens * heads, width)
    rotated = jnp.dot(flat, signs, preferred_element_type=jnp.float32)
    rotated = rotated * (1.0 / math.sqrt(half))
    for w in range(2):
        rot_scr[w] = rotated[:, w * half : (w + 1) * half]
    found = []
    for j in range(heads):
        parts = []
        for w in range(2):
            own = rot_scr[w, pl.ds(j, tokens, stride=heads), :] if heads > 1 else rot_scr[w]
            parts.append(jnp.clip(own / scale_of(j, w), -448.0, 448.0).astype(jnp.bfloat16))
        found.append(parts)
    return found


def page_places(slots_ref, ctx_id, tokens):
    pages = slots_ref.shape[1]
    row = lax.broadcasted_iota(jnp.int32, (tokens, pages), 0)
    page = lax.broadcasted_iota(jnp.int32, (tokens, pages), 1)
    slot = ctx_id * (tokens // BLK) + (row >> 4)
    place = (page * BLK + (row & (BLK - 1))).astype(jnp.float32)
    hit = jnp.broadcast_to(slots_ref[...], (tokens, pages)) == slot
    return jnp.sum(jnp.where(hit, place, 0.0), axis=1, keepdims=True)


def picker(distance, offset, count):
    key = lax.broadcasted_iota(jnp.int32, distance.shape, 1)
    hit = (distance == offset.astype(jnp.float32)) & (key < count)
    return jnp.where(hit, 1.0, 0.0).astype(jnp.bfloat16)


def spans_of(count_refs, info_ref, steps, tokens):
    if info_ref is not None:
        return [(info_ref[i, 0], info_ref[i, 1]) for i in range(len(steps))]
    me = lax.axis_index("ctx")
    known = [ref[0:1, :][0, 0] for ref in count_refs]
    known.append(tokens * 3 - known[0] - known[1] - known[2])
    spans = []
    for step in steps:
        ident = me ^ step
        offset = jnp.int32(0)
        for other in range(4):
            offset = offset + jnp.where((me ^ other) < ident, known[other], 0)
        spans.append((offset, known[step]))
    return spans


def ready_kernel(*refs):
    sources, refs = refs[:6], refs[6:]
    ints_out, floats_out, signs_out, place_out, codes_out, query_ref, rot_scr = refs[:7]
    start_ref, scale_ref, count_ref, slots_ref, rows_ref, sems = refs[7:]
    held = (start_ref, scale_ref, count_ref, slots_ref, rows_ref, query_ref)
    copies = [pltpu.make_async_copy(a, b, sems.at[i]) for i, (a, b) in enumerate(zip(sources, held))]
    for copy in copies:
        copy.start()
    tokens, heads, width = rows_ref.shape
    sets, rows, _ = query_ref.shape
    ctx_id = lax.axis_index("ctx")
    rep_id = lax.axis_index("rep")
    pair_head = lax.axis_index("head") * lax.axis_size("rep") * heads
    signs = sign_pair(width)
    signs_out[...] = signs
    ints_out[...] = jnp.zeros(ints_out.shape, jnp.int32)
    floats_out[...] = jnp.zeros(floats_out.shape, jnp.float32)
    for copy in copies[:5]:
        copy.wait()
    ints_out[0:1, :] = jnp.full((1, 128), count_ref[0], jnp.int32)
    for c in range(sets):
        ints_out[1 + c : 2 + c, :] = jnp.full((1, 128), start_ref[c] + ctx_id * rows, jnp.int32)
    for side, member in enumerate((rep_id, 1 - rep_id)):
        for j in range(heads):
            for w in range(2):
                scale = scale_ref[w, pair_head + member * heads + j]
                at = (side * heads + j) * 2 + w
                floats_out[at : at + 1, :] = jnp.full((1, 128), scale, jnp.float32)
    place = jnp.broadcast_to(page_places(slots_ref, ctx_id, tokens), (tokens, tokens))
    token = lax.broadcasted_iota(jnp.int32, (tokens, tokens), 1)
    place_out[...] = place - token.astype(jnp.float32)
    found = codes_of(rows_ref, scale_reader(floats_out, 0, heads), signs, rot_scr)
    codes_out[...] = jnp.concatenate([part for parts in found for part in parts], axis=1)
    copies[5].wait()


def scale_reader(floats_ref, side, heads):
    def scale_of(j, w):
        at = (side * heads + j) * 2 + w
        return floats_ref[at : at + 1, :]

    return scale_of


def make_ready(starts, scales, counts, slots, rows, query):
    tokens, heads, width = rows.shape
    half = width // 2
    return pl.pallas_call(
        ready_kernel,
        out_shape=[
            jax.ShapeDtypeStruct((8, 128), jnp.int32),
            jax.ShapeDtypeStruct((8, 128), jnp.float32),
            jax.ShapeDtypeStruct((width, width), jnp.bfloat16),
            jax.ShapeDtypeStruct((tokens, tokens), jnp.float32),
            jax.ShapeDtypeStruct((tokens, heads * width), jnp.bfloat16),
            jax.ShapeDtypeStruct(query.shape, query.dtype),
        ],
        in_specs=[pl.BlockSpec(memory_space=pltpu.HBM)] * 6,
        out_specs=[VMEM_SPEC] * 6,
        scratch_shapes=[
            pltpu.VMEM((2, tokens * heads, half), jnp.float32),
            pltpu.SMEM(starts.shape, jnp.int32),
            pltpu.SMEM(scales.shape, jnp.float32),
            pltpu.SMEM(counts.shape, jnp.int32),
            pltpu.VMEM(slots.shape, jnp.int32),
            pltpu.VMEM(rows.shape, rows.dtype),
            pltpu.SemaphoreType.DMA((6,)),
        ],
        compiler_params=pltpu.CompilerParams(vmem_limit_bytes=VMEM_LIMIT),
        cost_estimate=pl.CostEstimate(
            flops=tokens * heads * width * width * 2, bytes_accessed=2 << 20, transcendentals=0
        ),
    )(starts, scales, counts, slots, rows, query)


def attend_kernel(metas, steps, with_codes, has_state, last, *refs):
    refs = list(refs)
    info_ref = refs.pop(0) if metas == 0 else None
    count_refs = [refs.pop(0) for _ in range(metas)]
    ints_ref, floats_ref, signs_ref, query_ref = [refs.pop(0) for _ in range(4)]
    codes_ref = refs.pop(0) if with_codes else None
    rows_refs = [refs.pop(0) for _ in range(len(steps) - with_codes)]
    state = [refs.pop(0) for _ in range(2)] if has_state else None
    place_ref = None if last else refs.pop(0)
    pick_ref, moved_ref = (refs.pop(0), refs.pop(0)) if last else (None, None)
    out_ref = refs.pop(0)
    level_out = None if last else refs.pop(0)
    moved_out = refs.pop(0)
    pick_out = refs.pop(0) if with_codes else None
    rot_scr = refs.pop(0)

    tokens, heads, width = rows_refs[0].shape
    half = width // 2
    sets, rows, query_width = query_ref.shape
    group = query_width // half // heads
    stack = group * rows
    shards = len(steps)
    spans = spans_of(count_refs, info_ref, steps, tokens)
    bases = [ints_ref[1 + c : 2 + c, :][0, 0] for c in range(sets)]
    scale_of = scale_reader(floats_ref, 0, heads)

    def shard_codes():
        per_shard = []
        if with_codes:
            per_shard.append(
                [
                    [codes_ref[:, (2 * j + w) * half : (2 * j + w + 1) * half] for w in range(2)]
                    for j in range(heads)
                ]
            )
        return per_shard + [codes_of(r, scale_of, signs_ref[...], rot_scr) for r in rows_refs]

    def operands(per_shard):
        def joined(j, w):
            parts = [found[j][w] for found in per_shard]
            return jnp.concatenate(parts, axis=0) if shards > 1 else parts[0]

        keys = [joined(j, 0) for j in range(heads)]
        ones = jnp.ones((shards * tokens, half), jnp.bfloat16)
        values = [jnp.concatenate([joined(j, 1), ones], axis=1) for j in range(heads)]
        row = lax.broadcasted_iota(jnp.int32, (tokens, half), 1)
        key = lax.broadcasted_iota(jnp.int32, (tokens, half), 0)
        masked_keys = []
        for c in range(sets):
            parts = []
            for offset, count in spans:
                counted = (key < count) & (key + (offset - bases[c]) <= row)
                parts.append(jnp.where(counted, 0.0, MASKED).astype(jnp.bfloat16))
            bias = jnp.concatenate(parts, axis=0) if shards > 1 else parts[0]
            masked_keys.append([jnp.concatenate([keys[j], bias], axis=1) for j in range(heads)])
        unit = (
            lax.broadcasted_iota(jnp.int32, (rows, half), 0)
            == lax.broadcasted_iota(jnp.int32, (rows, half), 1)
        )
        unit = jnp.where(unit, 1.0, 0.0).astype(jnp.bfloat16)
        return masked_keys, values, jnp.concatenate([unit] * group, axis=0)

    def scores_of(c, j, keys, units):
        stacked = jnp.concatenate(
            [
                query_ref[c, :, (j * group + g) * half : (j * group + g + 1) * half]
                for g in range(group)
            ],
            axis=0,
        )
        stacked = jnp.concatenate([stacked, units], axis=1)
        return lax.dot_general(
            stacked, keys[c][j], (((1,), (1,)), ((), ())), preferred_element_type=jnp.float32
        )

    def tiles(scores):
        for i in range(0, scores.shape[1], half):
            yield scores[:, i : min(i + half, scores.shape[1])]

    def compute_near(per_shard):
        keys, values, units = operands(per_shard)
        worst = jnp.zeros((8, half), jnp.float32)
        for c in range(sets):
            for j in range(heads):
                factor = scale_of(j, 0) * LOG2E
                level = state[1][c, j]
                probs = []
                for part in tiles(scores_of(c, j, keys, units)):
                    size = part.shape[1]
                    part = (part - level[:, :size]) * factor[:, :size]
                    probs.append(jnp.exp2(part).astype(jnp.bfloat16))
                weighted = jnp.dot(
                    jnp.concatenate(probs, axis=1), values[j], preferred_element_type=jnp.float32
                )
                total = weighted[:, half:]
                worst = jnp.maximum(worst, jnp.max(total.reshape(stack // 8, 8, half), axis=0))
                share = 1.0 / (total + 1.0)
                for g in range(group):
                    one = slice(g * rows, (g + 1) * rows)
                    cols = slice((j * group + g) * half, (j * group + g + 1) * half)
                    part = weighted[one, :half] * scale_of(j, 1)
                    part = (part + state[0][c, :, cols].astype(jnp.float32)) * share[one]
                    out_ref[c, :, cols] = part.astype(jnp.bfloat16)
        return jnp.max(worst)

    def compute(per_shard):
        keys, values, units = operands(per_shard)
        for c in range(sets):
            for j in range(heads):
                factor = scale_of(j, 0) * LOG2E
                scores = scores_of(c, j, keys, units)
                top = jnp.max(scores, axis=1, keepdims=True)
                top = jnp.broadcast_to(top, (stack, half))
                if has_state:
                    level = state[1][c, j]
                    top = jnp.maximum(top, level)
                else:
                    top = jnp.maximum(top, FLOOR)
                probs = []
                for part in tiles(scores):
                    size = part.shape[1]
                    part = jnp.exp2((part - top[:, :size]) * factor[:, :size])
                    probs.append(part.astype(jnp.bfloat16))
                weighted = jnp.dot(
                    jnp.concatenate(probs, axis=1), values[j], preferred_element_type=jnp.float32
                )
                acc = weighted[:, :half] * scale_of(j, 1)
                total = weighted[:, half:]
                if has_state:
                    alpha = jnp.exp2((level - top) * factor)
                    total = total + alpha
                else:
                    total = jnp.maximum(total, TINY)
                for g in range(group):
                    one = slice(g * rows, (g + 1) * rows)
                    cols = slice((j * group + g) * half, (j * group + g + 1) * half)
                    part = acc[one]
                    if has_state:
                        part = part + state[0][c, :, cols].astype(jnp.float32) * alpha[one]
                    out_ref[c, :, cols] = (part / total[one]).astype(jnp.bfloat16)
                if not last:
                    level_out[c, j] = top + jnp.log2(total) / factor

    def picked(pick, found):
        own = jnp.concatenate([part for parts in found for part in parts], axis=1)
        return jnp.dot(pick, own, preferred_element_type=jnp.float32)

    if last:

        def deliver(per_shard):
            total = picked(pick_ref[...], per_shard[0]) + moved_ref[...].astype(jnp.float32)
            moved_out[...] = total.astype(jnp.bfloat16)

        latest = bases[0]
        for base in bases[1:]:
            latest = jnp.maximum(latest, base)
        needed = spans[0][0] < latest + rows

        @pl.when(needed)
        def _():
            per_shard = shard_codes()
            worst = compute_near(per_shard)
            deliver(per_shard)

            @pl.when(worst > FAR)
            def _():
                compute(per_shard)

        @pl.when(jnp.logical_not(needed))
        def _():
            deliver(shard_codes())
            out_ref[...] = state[0][...]

    else:
        per_shard = shard_codes()
        compute(per_shard)
        place = place_ref[...]
        total = None
        for (offset, count), found in zip(spans, per_shard):
            part = picked(picker(place, offset, count), found)
            total = part if total is None else total + part
        if with_codes:
            ((offset, count),) = spans_of(count_refs, info_ref, (3,), tokens)
            pick_out[...] = picker(place, offset, count)
        moved_out[...] = total.astype(jnp.bfloat16)


def attend(counts, info, steps, ready, rows, codes=None, state=None, picked=None):
    ints, floats, signs, place, _, query = ready
    tokens, heads, width = rows[0].shape
    half = width // 2
    sets, query_rows, query_width = query.shape
    group = query_width // half // heads
    args = list(counts) if info is None else [info]
    specs = [VMEM_SPEC] * len(counts) if info is None else [SMEM_SPEC]
    args += [ints, floats, signs, query]
    if codes is not None:
        args.append(codes)
    args += rows
    if state is not None:
        args += list(state)
    last = picked is not None
    args += list(picked) if last else [place]
    specs += [VMEM_SPEC] * (len(args) - len(specs))
    outs = [jax.ShapeDtypeStruct(query.shape, jnp.bfloat16)]
    if not last:
        stacked = (sets, heads, group * query_rows, half)
        outs.append(jax.ShapeDtypeStruct(stacked, jnp.float32))
    outs.append(jax.ShapeDtypeStruct((tokens, heads * width), jnp.bfloat16))
    if codes is not None:
        outs.append(jax.ShapeDtypeStruct((tokens, tokens), jnp.bfloat16))
    keys = tokens * len(steps)
    work = sets * heads * group * query_rows * keys
    return pl.pallas_call(
        functools.partial(
            attend_kernel,
            len(counts) if info is None else 0,
            steps,
            codes is not None,
            state is not None,
            last,
        ),
        out_shape=outs,
        in_specs=specs,
        out_specs=[VMEM_SPEC] * len(outs),
        scratch_shapes=[pltpu.VMEM((2, tokens * heads, half), jnp.float32)],
        compiler_params=pltpu.CompilerParams(vmem_limit_bytes=VMEM_LIMIT),
        cost_estimate=pl.CostEstimate(
            flops=work * half * 8, bytes_accessed=4 << 20, transcendentals=work
        ),
    )(*args)


def finish_kernel(
    floats_ref, signs_ref, pick_ref, result_ref, own, other, other_rows, *outs_and_scratch
):
    attention_out, cache_out, rot_scr, cache_scr, sems = outs_and_scratch
    tokens, heads, width = other_rows.shape
    half = width // 2
    sets = result_ref.shape[0]
    rep_id = lax.axis_index("rep")
    sent = [
        pltpu.make_async_copy(result_ref.at[c], attention_out.at[c], sems.at[c]) for c in range(sets)
    ]
    for copy in sent:
        copy.start()
    scales = [scale_reader(floats_ref, side, heads) for side in range(2)]
    found = codes_of(other_rows, scales[1], signs_ref[...], rot_scr)
    pick = pick_ref[...]
    pieces = []
    start = 0
    for i, eighths in enumerate(PIECES):
        size = tokens // 12 * eighths
        here = pl.ds(start, size)
        pieces.append(
            (
                slice(start, start + size),
                pltpu.make_async_copy(cache_scr.at[here], cache_out.at[here], sems.at[sets + i]),
            )
        )
        start += size

    for turn in range(2):

        @pl.when(rep_id == turn)
        def _(turn=turn):
            for here, piece in pieces:
                for side, moved in enumerate((own, other)):
                    first = (side if turn == 0 else 1 - side) * heads
                    for j in range(heads):
                        for w in range(2):
                            cols = slice((2 * j + w) * half, (2 * j + w + 1) * half)
                            part = moved[here, cols].astype(jnp.float32)
                            if side == 1:
                                part = part + jnp.dot(
                                    pick[here], found[j][w], preferred_element_type=jnp.float32
                                )
                            part = part * scales[side](j, w)
                            cache_scr[here, first + j, w * half : (w + 1) * half] = part
                piece.start()

    for copy in sent + [piece for _, piece in pieces]:
        copy.wait()


def finish(ready, pick, result, own, other, other_rows):
    _, floats, signs, _, _, _ = ready
    tokens, heads, width = other_rows.shape
    cache = (tokens, 2 * heads, width)
    args = [floats, signs, pick, result, own, other, other_rows]
    return pl.pallas_call(
        finish_kernel,
        out_shape=[
            jax.ShapeDtypeStruct(result.shape, result.dtype),
            jax.ShapeDtypeStruct(cache, jnp.float32),
        ],
        in_specs=[VMEM_SPEC] * len(args),
        out_specs=[pl.BlockSpec(memory_space=pl.ANY)] * 2,
        scratch_shapes=[
            pltpu.VMEM((2, tokens * heads, width // 2), jnp.float32),
            pltpu.VMEM(cache, jnp.float32),
            pltpu.SemaphoreType.DMA((result.shape[0] + len(PIECES),)),
        ],
        compiler_params=pltpu.CompilerParams(vmem_limit_bytes=VMEM_LIMIT),
        cost_estimate=pl.CostEstimate(
            flops=tokens * tokens * heads * width * 4, bytes_accessed=2 << 20, transcendentals=0
        ),
    )(*args)


def pair(value, axis, step):
    size = lax.axis_size(axis)
    return lax.ppermute(value, axis, [(i, i ^ step) for i in range(size)])


def body(kv_rows, kv_scales, queries, shard_counts, span_starts, block_slots):
    across = pair(kv_rows, "ctx", 2)
    beside = pair(kv_rows, "ctx", 1)
    ready = make_ready(
        span_starts, kv_scales.T, shard_counts, block_slots[None, :], kv_rows, queries
    )
    count = jnp.broadcast_to(shard_counts[:, None], (8, 128))
    counts = [count, pair(count, "ctx", 1), pair(count, "ctx", 2)]
    corner = pair(across, "ctx", 1)
    *state, moved, pick = attend(counts, None, (0, 1, 2), ready, [beside, across], ready[4])
    moved_other = pair(moved, "rep", 1)
    corner_other = pair(corner, "rep", 1)
    result, own = attend(counts, None, (3,), ready, [corner], None, state, (pick, moved))
    return finish(ready, pick, result, own, moved_other, corner_other)


def body_any(kv_rows, kv_scales, queries, shard_counts, span_starts, block_slots):
    counts = lax.all_gather(shard_counts, "ctx", axis=0, tiled=True)
    info = jnp.stack([jnp.cumsum(counts) - counts, counts], axis=1)
    every = lax.all_gather(kv_rows, "ctx", axis=0)
    size = 4 if every.shape[0] % 4 == 0 else 1
    every = every.reshape(-1, size, *kv_rows.shape)
    info = info.reshape(-1, size, 2)
    ready = make_ready(
        span_starts, kv_scales.T, shard_counts, block_slots[None, :], kv_rows, queries
    )

    def take(some, rows, state=None):
        return attend([], some, (0,) * size, ready, [rows[i] for i in range(size)], None, state)

    def step(carry, turn):
        state, moved = carry
        rows, some = turn
        *state, found = take(some, rows, state)
        return (tuple(state), moved + found), None

    *state, moved = take(info[0], every[0])
    (state, moved), _ = lax.scan(step, (tuple(state), moved), (every[1:], info[1:]))
    none = jnp.zeros((kv_rows.shape[0],) * 2, jnp.bfloat16)
    return finish(ready, none, state[0], moved, pair(moved, "rep", 1), kv_rows)


def solution(mesh):
    in_specs = (
        P(("groups", "ctx"), ("head", "rep"), None),
        P(),
        P(None, ("groups", "ctx"), ("head", "rep")),
        P(("groups", "ctx")),
        P("groups"),
        P("groups"),
    )
    out_specs = (P(None, ("groups", "ctx"), ("head", "rep")), P(("groups", "ctx"), "head", None))
    chosen = body if mesh.shape["ctx"] == 4 else body_any
    return jax.shard_map(chosen, mesh=mesh, in_specs=in_specs, out_specs=out_specs, check_vma=False)
```

```python
import functools
import math

import jax
import jax.numpy as jnp
from jax import lax
from jax.experimental import pallas as pl
from jax.experimental.pallas import tpu as pltpu
from jax.sharding import PartitionSpec as P

BLK = 16
FLOOR = -1e9
MASKED = -1e30
TINY = 1e-30
FAR = 2.0**60
PIECES = (6, 4, 2)
LOG2E = math.log2(math.e)
VMEM_LIMIT = 48 * 1024 * 1024
SMEM_SPEC = pl.BlockSpec(memory_space=pltpu.SMEM)
VMEM_SPEC = pl.BlockSpec(memory_space=pltpu.VMEM)


def sign_pair(width):
    half = width // 2
    row = lax.broadcasted_iota(jnp.int32, (width, width), 0)
    col = lax.broadcasted_iota(jnp.int32, (width, width), 1)
    parity = row & col & (half - 1)
    parity = parity ^ (parity >> 4)
    parity = parity ^ (parity >> 2)
    parity = (parity ^ (parity >> 1)) & 1
    same = (row >= half) == (col >= half)
    return jnp.where(same, (1 - 2 * parity).astype(jnp.float32), 0.0).astype(jnp.bfloat16)


def codes_of(rows_ref, scale_of, signs, rot_scr):
    tokens, heads, width = rows_ref.shape
    half = width // 2
    flat = rows_ref[...].reshape(tokens * heads, width)
    rotated = jnp.dot(flat, signs, preferred_element_type=jnp.float32)
    rotated = rotated * (1.0 / math.sqrt(half))
    for w in range(2):
        rot_scr[w] = rotated[:, w * half : (w + 1) * half]
    found = []
    for j in range(heads):
        parts = []
        for w in range(2):
            own = rot_scr[w, pl.ds(j, tokens, stride=heads), :] if heads > 1 else rot_scr[w]
            parts.append(jnp.clip(own / scale_of(j, w), -448.0, 448.0).astype(jnp.bfloat16))
        found.append(parts)
    return found


def page_places(slots_ref, ctx_id, tokens):
    pages = slots_ref.shape[1]
    row = lax.broadcasted_iota(jnp.int32, (tokens, pages), 0)
    page = lax.broadcasted_iota(jnp.int32, (tokens, pages), 1)
    slot = ctx_id * (tokens // BLK) + (row >> 4)
    place = (page * BLK + (row & (BLK - 1))).astype(jnp.float32)
    hit = jnp.broadcast_to(slots_ref[...], (tokens, pages)) == slot
    return jnp.sum(jnp.where(hit, place, 0.0), axis=1, keepdims=True)


def picker(distance, offset, count):
    key = lax.broadcasted_iota(jnp.int32, distance.shape, 1)
    hit = (distance == offset.astype(jnp.float32)) & (key < count)
    return jnp.where(hit, 1.0, 0.0).astype(jnp.bfloat16)


def spans_of(count_refs, info_ref, steps, tokens):
    if info_ref is not None:
        return [(info_ref[i, 0], info_ref[i, 1]) for i in range(len(steps))]
    me = lax.axis_index("ctx")
    known = [ref[0:1, :][0, 0] for ref in count_refs]
    known.append(tokens * 3 - known[0] - known[1] - known[2])
    spans = []
    for step in steps:
        ident = me ^ step
        offset = jnp.int32(0)
        for other in range(4):
            offset = offset + jnp.where((me ^ other) < ident, known[other], 0)
        spans.append((offset, known[step]))
    return spans


def ready_kernel(*refs):
    sources, refs = refs[:6], refs[6:]
    ints_out, floats_out, signs_out, place_out, codes_out, query_ref, rot_scr = refs[:7]
    start_ref, scale_ref, count_ref, slots_ref, rows_ref, sems = refs[7:]
    held = (start_ref, scale_ref, count_ref, slots_ref, rows_ref, query_ref)
    copies = [pltpu.make_async_copy(a, b, sems.at[i]) for i, (a, b) in enumerate(zip(sources, held))]
    for copy in copies:
        copy.start()
    tokens, heads, width = rows_ref.shape
    sets, rows, _ = query_ref.shape
    ctx_id = lax.axis_index("ctx")
    rep_id = lax.axis_index("rep")
    pair_head = lax.axis_index("head") * lax.axis_size("rep") * heads
    signs = sign_pair(width)
    signs_out[...] = signs
    ints_out[...] = jnp.zeros(ints_out.shape, jnp.int32)
    floats_out[...] = jnp.zeros(floats_out.shape, jnp.float32)
    for copy in copies[:5]:
        copy.wait()
    ints_out[0:1, :] = jnp.full((1, 128), count_ref[0], jnp.int32)
    for c in range(sets):
        ints_out[1 + c : 2 + c, :] = jnp.full((1, 128), start_ref[c] + ctx_id * rows, jnp.int32)
    for side, member in enumerate((rep_id, 1 - rep_id)):
        for j in range(heads):
            for w in range(2):
                scale = scale_ref[w, pair_head + member * heads + j]
                at = (side * heads + j) * 2 + w
                floats_out[at : at + 1, :] = jnp.full((1, 128), scale, jnp.float32)
    place = jnp.broadcast_to(page_places(slots_ref, ctx_id, tokens), (tokens, tokens))
    token = lax.broadcasted_iota(jnp.int32, (tokens, tokens), 1)
    place_out[...] = place - token.astype(jnp.float32)
    found = codes_of(rows_ref, scale_reader(floats_out, 0, heads), signs, rot_scr)
    codes_out[...] = jnp.concatenate([part for parts in found for part in parts], axis=1)
    copies[5].wait()


def scale_reader(floats_ref, side, heads):
    def scale_of(j, w):
        at = (side * heads + j) * 2 + w
        return floats_ref[at : at + 1, :]

    return scale_of


def make_ready(starts, scales, counts, slots, rows, query):
    tokens, heads, width = rows.shape
    half = width // 2
    return pl.pallas_call(
        ready_kernel,
        out_shape=[
            jax.ShapeDtypeStruct((8, 128), jnp.int32),
            jax.ShapeDtypeStruct((8, 128), jnp.float32),
            jax.ShapeDtypeStruct((width, width), jnp.bfloat16),
            jax.ShapeDtypeStruct((tokens, tokens), jnp.float32),
            jax.ShapeDtypeStruct((tokens, heads * width), jnp.bfloat16),
            jax.ShapeDtypeStruct(query.shape, query.dtype),
        ],
        in_specs=[pl.BlockSpec(memory_space=pltpu.HBM)] * 6,
        out_specs=[VMEM_SPEC] * 6,
        scratch_shapes=[
            pltpu.VMEM((2, tokens * heads, half), jnp.float32),
            pltpu.SMEM(starts.shape, jnp.int32),
            pltpu.SMEM(scales.shape, jnp.float32),
            pltpu.SMEM(counts.shape, jnp.int32),
            pltpu.VMEM(slots.shape, jnp.int32),
            pltpu.VMEM(rows.shape, rows.dtype),
            pltpu.SemaphoreType.DMA((6,)),
        ],
        compiler_params=pltpu.CompilerParams(vmem_limit_bytes=VMEM_LIMIT),
        cost_estimate=pl.CostEstimate(
            flops=tokens * heads * width * width * 2, bytes_accessed=2 << 20, transcendentals=0
        ),
    )(starts, scales, counts, slots, rows, query)


def attend_kernel(metas, steps, with_codes, has_state, last, *refs):
    refs = list(refs)
    info_ref = refs.pop(0) if metas == 0 else None
    count_refs = [refs.pop(0) for _ in range(metas)]
    ints_ref, floats_ref, signs_ref, query_ref = [refs.pop(0) for _ in range(4)]
    codes_ref = refs.pop(0) if with_codes else None
    rows_refs = [refs.pop(0) for _ in range(len(steps) - with_codes)]
    state = [refs.pop(0) for _ in range(2)] if has_state else None
    place_ref = None if last else refs.pop(0)
    pick_ref, moved_ref = (refs.pop(0), refs.pop(0)) if last else (None, None)
    out_ref = refs.pop(0)
    level_out = None if last else refs.pop(0)
    moved_out = refs.pop(0)
    pick_out = refs.pop(0) if with_codes else None
    rot_scr = refs.pop(0)

    tokens, heads, width = rows_refs[0].shape
    half = width // 2
    sets, rows, query_width = query_ref.shape
    group = query_width // half // heads
    stack = group * rows
    shards = len(steps)
    spans = spans_of(count_refs, info_ref, steps, tokens)
    bases = [ints_ref[1 + c : 2 + c, :][0, 0] for c in range(sets)]
    scale_of = scale_reader(floats_ref, 0, heads)

    def shard_codes():
        per_shard = []
        if with_codes:
            per_shard.append(
                [
                    [codes_ref[:, (2 * j + w) * half : (2 * j + w + 1) * half] for w in range(2)]
                    for j in range(heads)
                ]
            )
        return per_shard + [codes_of(r, scale_of, signs_ref[...], rot_scr) for r in rows_refs]

    def operands(per_shard):
        def joined(j, w):
            parts = [found[j][w] for found in per_shard]
            return jnp.concatenate(parts, axis=0) if shards > 1 else parts[0]

        keys = [joined(j, 0) for j in range(heads)]
        ones = jnp.ones((shards * tokens, half), jnp.bfloat16)
        values = [jnp.concatenate([joined(j, 1), ones], axis=1) for j in range(heads)]
        if not last:
            row = lax.broadcasted_iota(jnp.int32, (rows, tokens), 0)
            key = lax.broadcasted_iota(jnp.int32, (rows, tokens), 1)
            biases = []
            for c in range(sets):
                parts = []
                for offset, count in spans:
                    counted = (key < count) & (key + (offset - bases[c]) <= row)
                    parts.append(jnp.where(counted, 0.0, MASKED))
                bias = jnp.concatenate(parts, axis=1) if shards > 1 else parts[0]
                biases.append(jnp.concatenate([bias] * group, axis=0))
            return [keys] * sets, values, biases
        row = lax.broadcasted_iota(jnp.int32, (tokens, half), 1)
        key = lax.broadcasted_iota(jnp.int32, (tokens, half), 0)
        masked_keys = []
        for c in range(sets):
            parts = []
            for offset, count in spans:
                counted = (key < count) & (key + (offset - bases[c]) <= row)
                parts.append(jnp.where(counted, 0.0, MASKED).astype(jnp.bfloat16))
            bias = jnp.concatenate(parts, axis=0) if shards > 1 else parts[0]
            masked_keys.append([jnp.concatenate([keys[j], bias], axis=1) for j in range(heads)])
        unit = (
            lax.broadcasted_iota(jnp.int32, (rows, half), 0)
            == lax.broadcasted_iota(jnp.int32, (rows, half), 1)
        )
        unit = jnp.where(unit, 1.0, 0.0).astype(jnp.bfloat16)
        return masked_keys, values, jnp.concatenate([unit] * group, axis=0)

    def scores_of(c, j, keys, units):
        stacked = jnp.concatenate(
            [
                query_ref[c, :, (j * group + g) * half : (j * group + g + 1) * half]
                for g in range(group)
            ],
            axis=0,
        )
        if last:
            stacked = jnp.concatenate([stacked, units], axis=1)
        scores = lax.dot_general(
            stacked, keys[c][j], (((1,), (1,)), ((), ())), preferred_element_type=jnp.float32
        )
        return scores if last else scores + units[c]

    def tiles(scores):
        for i in range(0, scores.shape[1], half):
            yield scores[:, i : min(i + half, scores.shape[1])]

    def compute_near(per_shard):
        keys, values, units = operands(per_shard)
        worst = jnp.zeros((8, half), jnp.float32)
        for c in range(sets):
            for j in range(heads):
                factor = scale_of(j, 0) * LOG2E
                level = state[1][c, j]
                probs = []
                for part in tiles(scores_of(c, j, keys, units)):
                    size = part.shape[1]
                    part = (part - level[:, :size]) * factor[:, :size]
                    probs.append(jnp.exp2(part).astype(jnp.bfloat16))
                weighted = jnp.dot(
                    jnp.concatenate(probs, axis=1), values[j], preferred_element_type=jnp.float32
                )
                total = weighted[:, half:]
                worst = jnp.maximum(worst, jnp.max(total.reshape(stack // 8, 8, half), axis=0))
                share = 1.0 / (total + 1.0)
                for g in range(group):
                    one = slice(g * rows, (g + 1) * rows)
                    cols = slice((j * group + g) * half, (j * group + g + 1) * half)
                    part = weighted[one, :half] * scale_of(j, 1)
                    part = (part + state[0][c, :, cols].astype(jnp.float32)) * share[one]
                    out_ref[c, :, cols] = part.astype(jnp.bfloat16)
        return jnp.max(worst)

    def compute(per_shard):
        keys, values, units = operands(per_shard)
        for c in range(sets):
            for j in range(heads):
                factor = scale_of(j, 0) * LOG2E
                scores = scores_of(c, j, keys, units)
                top = jnp.max(scores, axis=1, keepdims=True)
                top = jnp.broadcast_to(top, (stack, half))
                if has_state:
                    level = state[1][c, j]
                    top = jnp.maximum(top, level)
                else:
                    top = jnp.maximum(top, FLOOR)
                probs = []
                for part in tiles(scores):
                    size = part.shape[1]
                    part = jnp.exp2((part - top[:, :size]) * factor[:, :size])
                    probs.append(part.astype(jnp.bfloat16))
                weighted = jnp.dot(
                    jnp.concatenate(probs, axis=1), values[j], preferred_element_type=jnp.float32
                )
                acc = weighted[:, :half] * scale_of(j, 1)
                total = weighted[:, half:]
                if has_state:
                    alpha = jnp.exp2((level - top) * factor)
                    total = total + alpha
                else:
                    total = jnp.maximum(total, TINY)
                for g in range(group):
                    one = slice(g * rows, (g + 1) * rows)
                    cols = slice((j * group + g) * half, (j * group + g + 1) * half)
                    part = acc[one]
                    if has_state:
                        part = part + state[0][c, :, cols].astype(jnp.float32) * alpha[one]
                    out_ref[c, :, cols] = (part / total[one]).astype(jnp.bfloat16)
                if not last:
                    level_out[c, j] = top + jnp.log2(total) / factor

    def picked(pick, found):
        own = jnp.concatenate([part for parts in found for part in parts], axis=1)
        return jnp.dot(pick, own, preferred_element_type=jnp.float32)

    if last:

        def deliver(per_shard):
            total = picked(pick_ref[...], per_shard[0]) + moved_ref[...].astype(jnp.float32)
            moved_out[...] = total.astype(jnp.bfloat16)

        latest = bases[0]
        for base in bases[1:]:
            latest = jnp.maximum(latest, base)
        needed = spans[0][0] < latest + rows

        @pl.when(needed)
        def _():
            per_shard = shard_codes()
            worst = compute_near(per_shard)
            deliver(per_shard)

            @pl.when(worst > FAR)
            def _():
                compute(per_shard)

        @pl.when(jnp.logical_not(needed))
        def _():
            deliver(shard_codes())
            out_ref[...] = state[0][...]

    else:
        per_shard = shard_codes()
        compute(per_shard)
        place = place_ref[...]
        total = None
        for (offset, count), found in zip(spans, per_shard):
            part = picked(picker(place, offset, count), found)
            total = part if total is None else total + part
        if with_codes:
            ((offset, count),) = spans_of(count_refs, info_ref, (3,), tokens)
            pick_out[...] = picker(place, offset, count)
        moved_out[...] = total.astype(jnp.bfloat16)


def attend(counts, info, steps, ready, rows, codes=None, state=None, picked=None):
    ints, floats, signs, place, _, query = ready
    tokens, heads, width = rows[0].shape
    half = width // 2
    sets, query_rows, query_width = query.shape
    group = query_width // half // heads
    args = list(counts) if info is None else [info]
    specs = [VMEM_SPEC] * len(counts) if info is None else [SMEM_SPEC]
    args += [ints, floats, signs, query]
    if codes is not None:
        args.append(codes)
    args += rows
    if state is not None:
        args += list(state)
    last = picked is not None
    args += list(picked) if last else [place]
    specs += [VMEM_SPEC] * (len(args) - len(specs))
    outs = [jax.ShapeDtypeStruct(query.shape, jnp.bfloat16)]
    if not last:
        stacked = (sets, heads, group * query_rows, half)
        outs.append(jax.ShapeDtypeStruct(stacked, jnp.float32))
    outs.append(jax.ShapeDtypeStruct((tokens, heads * width), jnp.bfloat16))
    if codes is not None:
        outs.append(jax.ShapeDtypeStruct((tokens, tokens), jnp.bfloat16))
    keys = tokens * len(steps)
    work = sets * heads * group * query_rows * keys
    return pl.pallas_call(
        functools.partial(
            attend_kernel,
            len(counts) if info is None else 0,
            steps,
            codes is not None,
            state is not None,
            last,
        ),
        out_shape=outs,
        in_specs=specs,
        out_specs=[VMEM_SPEC] * len(outs),
        scratch_shapes=[pltpu.VMEM((2, tokens * heads, half), jnp.float32)],
        compiler_params=pltpu.CompilerParams(vmem_limit_bytes=VMEM_LIMIT),
        cost_estimate=pl.CostEstimate(
            flops=work * half * 8, bytes_accessed=4 << 20, transcendentals=work
        ),
    )(*args)


def finish_kernel(
    floats_ref, signs_ref, pick_ref, result_ref, own, other, other_rows, *outs_and_scratch
):
    attention_out, cache_out, rot_scr, cache_scr, sems = outs_and_scratch
    tokens, heads, width = other_rows.shape
    half = width // 2
    sets = result_ref.shape[0]
    rep_id = lax.axis_index("rep")
    sent = [
        pltpu.make_async_copy(result_ref.at[c], attention_out.at[c], sems.at[c]) for c in range(sets)
    ]
    for copy in sent:
        copy.start()
    scales = [scale_reader(floats_ref, side, heads) for side in range(2)]
    found = codes_of(other_rows, scales[1], signs_ref[...], rot_scr)
    both = jnp.concatenate([part for parts in found for part in parts], axis=1)
    pick = pick_ref[...]
    pieces = []
    start = 0
    for i, eighths in enumerate(PIECES):
        size = tokens // 12 * eighths
        here = pl.ds(start, size)
        pieces.append(
            (
                slice(start, start + size),
                pltpu.make_async_copy(cache_scr.at[here], cache_out.at[here], sems.at[sets + i]),
            )
        )
        start += size

    for turn in range(2):

        @pl.when(rep_id == turn)
        def _(turn=turn):
            for here, piece in pieces:
                for side, moved in enumerate((own, other)):
                    first = (side if turn == 0 else 1 - side) * heads
                    if side == 1:
                        added = jnp.dot(pick[here], both, preferred_element_type=jnp.float32)
                    for j in range(heads):
                        for w in range(2):
                            cols = slice((2 * j + w) * half, (2 * j + w + 1) * half)
                            part = moved[here, cols].astype(jnp.float32)
                            if side == 1:
                                part = part + added[:, cols]
                            part = part * scales[side](j, w)
                            cache_scr[here, first + j, w * half : (w + 1) * half] = part
                piece.start()

    for copy in sent + [piece for _, piece in pieces]:
        copy.wait()


def finish(ready, pick, result, own, other, other_rows):
    _, floats, signs, _, _, _ = ready
    tokens, heads, width = other_rows.shape
    cache = (tokens, 2 * heads, width)
    args = [floats, signs, pick, result, own, other, other_rows]
    return pl.pallas_call(
        finish_kernel,
        out_shape=[
            jax.ShapeDtypeStruct(result.shape, result.dtype),
            jax.ShapeDtypeStruct(cache, jnp.float32),
        ],
        in_specs=[VMEM_SPEC] * len(args),
        out_specs=[pl.BlockSpec(memory_space=pl.ANY)] * 2,
        scratch_shapes=[
            pltpu.VMEM((2, tokens * heads, width // 2), jnp.float32),
            pltpu.VMEM(cache, jnp.float32),
            pltpu.SemaphoreType.DMA((result.shape[0] + len(PIECES),)),
        ],
        compiler_params=pltpu.CompilerParams(vmem_limit_bytes=VMEM_LIMIT),
        cost_estimate=pl.CostEstimate(
            flops=tokens * tokens * heads * width * 4, bytes_accessed=2 << 20, transcendentals=0
        ),
    )(*args)


def pair(value, axis, step):
    size = lax.axis_size(axis)
    return lax.ppermute(value, axis, [(i, i ^ step) for i in range(size)])


def body(kv_rows, kv_scales, queries, shard_counts, span_starts, block_slots):
    across = pair(kv_rows, "ctx", 2)
    beside = pair(kv_rows, "ctx", 1)
    ready = make_ready(
        span_starts, kv_scales.T, shard_counts, block_slots[None, :], kv_rows, queries
    )
    count = jnp.broadcast_to(shard_counts[:, None], (8, 128))
    counts = [count, pair(count, "ctx", 1), pair(count, "ctx", 2)]
    corner = pair(across, "ctx", 1)
    *state, moved, pick = attend(counts, None, (0, 1, 2), ready, [beside, across], ready[4])
    moved_other = pair(moved, "rep", 1)
    corner_other = pair(corner, "rep", 1)
    result, own = attend(counts, None, (3,), ready, [corner], None, state, (pick, moved))
    return finish(ready, pick, result, own, moved_other, corner_other)


def body_any(kv_rows, kv_scales, queries, shard_counts, span_starts, block_slots):
    counts = lax.all_gather(shard_counts, "ctx", axis=0, tiled=True)
    info = jnp.stack([jnp.cumsum(counts) - counts, counts], axis=1)
    every = lax.all_gather(kv_rows, "ctx", axis=0)
    size = 4 if every.shape[0] % 4 == 0 else 1
    every = every.reshape(-1, size, *kv_rows.shape)
    info = info.reshape(-1, size, 2)
    ready = make_ready(
        span_starts, kv_scales.T, shard_counts, block_slots[None, :], kv_rows, queries
    )

    def take(some, rows, state=None):
        return attend([], some, (0,) * size, ready, [rows[i] for i in range(size)], None, state)

    def step(carry, turn):
        state, moved = carry
        rows, some = turn
        *state, found = take(some, rows, state)
        return (tuple(state), moved + found), None

    *state, moved = take(info[0], every[0])
    (state, moved), _ = lax.scan(step, (tuple(state), moved), (every[1:], info[1:]))
    none = jnp.zeros((kv_rows.shape[0],) * 2, jnp.bfloat16)
    return finish(ready, none, state[0], moved, pair(moved, "rep", 1), kv_rows)


def solution(mesh):
    in_specs = (
        P(("groups", "ctx"), ("head", "rep"), None),
        P(),
        P(None, ("groups", "ctx"), ("head", "rep")),
        P(("groups", "ctx")),
        P("groups"),
        P("groups"),
    )
    out_specs = (P(None, ("groups", "ctx"), ("head", "rep")), P(("groups", "ctx"), "head", None))
    chosen = body if mesh.shape["ctx"] == 4 else body_any
    return jax.shard_map(chosen, mesh=mesh, in_specs=in_specs, out_specs=out_specs, check_vma=False)
```

```python
import functools
import math

import jax
import jax.numpy as jnp
from jax import lax
from jax.experimental import pallas as pl
from jax.experimental.pallas import tpu as pltpu
from jax.sharding import PartitionSpec as P

BLK = 16
FLOOR = -1e9
MASKED = -1e30
TINY = 1e-30
FAR = 2.0**60
PIECES = (6, 4, 2)
LOG2E = math.log2(math.e)
VMEM_LIMIT = 48 * 1024 * 1024
SMEM_SPEC = pl.BlockSpec(memory_space=pltpu.SMEM)
VMEM_SPEC = pl.BlockSpec(memory_space=pltpu.VMEM)


def sign_pair(width):
    half = width // 2
    row = lax.broadcasted_iota(jnp.int32, (width, width), 0)
    col = lax.broadcasted_iota(jnp.int32, (width, width), 1)
    parity = row & col & (half - 1)
    parity = parity ^ (parity >> 4)
    parity = parity ^ (parity >> 2)
    parity = (parity ^ (parity >> 1)) & 1
    same = (row >= half) == (col >= half)
    return jnp.where(same, (1 - 2 * parity).astype(jnp.float32), 0.0).astype(jnp.bfloat16)


def codes_of(rows_ref, scale_of, signs, rot_scr):
    tokens, heads, width = rows_ref.shape
    half = width // 2
    flat = rows_ref[...].reshape(tokens * heads, width)
    rotated = jnp.dot(flat, signs, preferred_element_type=jnp.float32)
    rotated = rotated * (1.0 / math.sqrt(half))
    for w in range(2):
        rot_scr[w] = rotated[:, w * half : (w + 1) * half]
    found = []
    for j in range(heads):
        parts = []
        for w in range(2):
            own = rot_scr[w, pl.ds(j, tokens, stride=heads), :] if heads > 1 else rot_scr[w]
            parts.append(jnp.clip(own / scale_of(j, w), -448.0, 448.0).astype(jnp.bfloat16))
        found.append(parts)
    return found


def page_places(slots_ref, ctx_id, tokens):
    pages = slots_ref.shape[1]
    row = lax.broadcasted_iota(jnp.int32, (tokens, pages), 0)
    page = lax.broadcasted_iota(jnp.int32, (tokens, pages), 1)
    slot = ctx_id * (tokens // BLK) + (row >> 4)
    place = (page * BLK + (row & (BLK - 1))).astype(jnp.float32)
    hit = jnp.broadcast_to(slots_ref[...], (tokens, pages)) == slot
    return jnp.sum(jnp.where(hit, place, 0.0), axis=1, keepdims=True)


def picker(distance, offset, count):
    key = lax.broadcasted_iota(jnp.int32, distance.shape, 1)
    hit = (distance == offset.astype(jnp.float32)) & (key < count)
    return jnp.where(hit, 1.0, 0.0).astype(jnp.bfloat16)


def spans_of(count_refs, info_ref, steps, tokens):
    if info_ref is not None:
        return [(info_ref[i, 0], info_ref[i, 1]) for i in range(len(steps))]
    me = lax.axis_index("ctx")
    known = [ref[0:1, :][0, 0] for ref in count_refs]
    known.append(tokens * 3 - known[0] - known[1] - known[2])
    spans = []
    for step in steps:
        ident = me ^ step
        offset = jnp.int32(0)
        for other in range(4):
            offset = offset + jnp.where((me ^ other) < ident, known[other], 0)
        spans.append((offset, known[step]))
    return spans


def ready_kernel(*refs):
    sources, refs = refs[:6], refs[6:]
    ints_out, floats_out, signs_out, place_out, codes_out, query_ref, rot_scr = refs[:7]
    start_ref, scale_ref, count_ref, slots_ref, rows_ref, sems = refs[7:]
    held = (start_ref, scale_ref, count_ref, slots_ref, rows_ref, query_ref)
    copies = [pltpu.make_async_copy(a, b, sems.at[i]) for i, (a, b) in enumerate(zip(sources, held))]
    for copy in copies:
        copy.start()
    tokens, heads, width = rows_ref.shape
    sets, rows, _ = query_ref.shape
    ctx_id = lax.axis_index("ctx")
    rep_id = lax.axis_index("rep")
    pair_head = lax.axis_index("head") * lax.axis_size("rep") * heads
    signs = sign_pair(width)
    signs_out[...] = signs
    ints_out[...] = jnp.zeros(ints_out.shape, jnp.int32)
    floats_out[...] = jnp.zeros(floats_out.shape, jnp.float32)
    for copy in copies[:5]:
        copy.wait()
    ints_out[0:1, :] = jnp.full((1, 128), count_ref[0], jnp.int32)
    for c in range(sets):
        ints_out[1 + c : 2 + c, :] = jnp.full((1, 128), start_ref[c] + ctx_id * rows, jnp.int32)
    for side, member in enumerate((rep_id, 1 - rep_id)):
        for j in range(heads):
            for w in range(2):
                scale = scale_ref[w, pair_head + member * heads + j]
                at = (side * heads + j) * 2 + w
                floats_out[at : at + 1, :] = jnp.full((1, 128), scale, jnp.float32)
    place = jnp.broadcast_to(page_places(slots_ref, ctx_id, tokens), (tokens, tokens))
    token = lax.broadcasted_iota(jnp.int32, (tokens, tokens), 1)
    place_out[...] = place - token.astype(jnp.float32)
    found = codes_of(rows_ref, scale_reader(floats_out, 0, heads), signs, rot_scr)
    codes_out[...] = jnp.concatenate([part for parts in found for part in parts], axis=1)
    copies[5].wait()


def scale_reader(floats_ref, side, heads):
    def scale_of(j, w):
        at = (side * heads + j) * 2 + w
        return floats_ref[at : at + 1, :]

    return scale_of


def make_ready(starts, scales, counts, slots, rows, query):
    tokens, heads, width = rows.shape
    half = width // 2
    return pl.pallas_call(
        ready_kernel,
        out_shape=[
            jax.ShapeDtypeStruct((8, 128), jnp.int32),
            jax.ShapeDtypeStruct((8, 128), jnp.float32),
            jax.ShapeDtypeStruct((width, width), jnp.bfloat16),
            jax.ShapeDtypeStruct((tokens, tokens), jnp.float32),
            jax.ShapeDtypeStruct((tokens, heads * width), jnp.bfloat16),
            jax.ShapeDtypeStruct(query.shape, query.dtype),
        ],
        in_specs=[pl.BlockSpec(memory_space=pltpu.HBM)] * 6,
        out_specs=[VMEM_SPEC] * 6,
        scratch_shapes=[
            pltpu.VMEM((2, tokens * heads, half), jnp.float32),
            pltpu.SMEM(starts.shape, jnp.int32),
            pltpu.SMEM(scales.shape, jnp.float32),
            pltpu.SMEM(counts.shape, jnp.int32),
            pltpu.VMEM(slots.shape, jnp.int32),
            pltpu.VMEM(rows.shape, rows.dtype),
            pltpu.SemaphoreType.DMA((6,)),
        ],
        compiler_params=pltpu.CompilerParams(vmem_limit_bytes=VMEM_LIMIT),
        cost_estimate=pl.CostEstimate(
            flops=tokens * heads * width * width * 2, bytes_accessed=2 << 20, transcendentals=0
        ),
    )(starts, scales, counts, slots, rows, query)


def attend_kernel(metas, steps, with_codes, has_state, last, *refs):
    refs = list(refs)
    info_ref = refs.pop(0) if metas == 0 else None
    count_refs = [refs.pop(0) for _ in range(metas)]
    ints_ref, floats_ref, signs_ref, query_ref = [refs.pop(0) for _ in range(4)]
    codes_ref = refs.pop(0) if with_codes else None
    rows_refs = [refs.pop(0) for _ in range(len(steps) - with_codes)]
    state = [refs.pop(0) for _ in range(2)] if has_state else None
    place_ref = None if last else refs.pop(0)
    pick_ref, moved_ref = (refs.pop(0), refs.pop(0)) if last else (None, None)
    out_ref = refs.pop(0)
    level_out = None if last else refs.pop(0)
    moved_out = refs.pop(0)
    pick_out = refs.pop(0) if with_codes else None
    rot_scr = refs.pop(0)

    tokens, heads, width = rows_refs[0].shape
    half = width // 2
    sets, rows, query_width = query_ref.shape
    group = query_width // half // heads
    stack = group * rows
    shards = len(steps)
    spans = spans_of(count_refs, info_ref, steps, tokens)
    bases = [ints_ref[1 + c : 2 + c, :][0, 0] for c in range(sets)]
    scale_of = scale_reader(floats_ref, 0, heads)

    def shard_codes():
        per_shard = []
        if with_codes:
            per_shard.append(
                [
                    [codes_ref[:, (2 * j + w) * half : (2 * j + w + 1) * half] for w in range(2)]
                    for j in range(heads)
                ]
            )
        return per_shard + [codes_of(r, scale_of, signs_ref[...], rot_scr) for r in rows_refs]

    def operands(per_shard):
        def joined(j, w):
            parts = [found[j][w] for found in per_shard]
            return jnp.concatenate(parts, axis=0) if shards > 1 else parts[0]

        keys = [joined(j, 0) for j in range(heads)]
        ones = jnp.ones((shards * tokens, half), jnp.bfloat16)
        values = [jnp.concatenate([joined(j, 1), ones], axis=1) for j in range(heads)]
        if not last:
            row = lax.broadcasted_iota(jnp.int32, (rows, tokens), 0)
            key = lax.broadcasted_iota(jnp.int32, (rows, tokens), 1)
            biases = []
            for c in range(sets):
                parts = []
                for offset, count in spans:
                    counted = (key < count) & (key + (offset - bases[c]) <= row)
                    parts.append(jnp.where(counted, 0.0, MASKED))
                bias = jnp.concatenate(parts, axis=1) if shards > 1 else parts[0]
                biases.append(jnp.concatenate([bias] * group, axis=0))
            return [keys] * sets, values, biases
        row = lax.broadcasted_iota(jnp.int32, (tokens, half), 1)
        key = lax.broadcasted_iota(jnp.int32, (tokens, half), 0)
        masked_keys = []
        for c in range(sets):
            parts = []
            for offset, count in spans:
                counted = (key < count) & (key + (offset - bases[c]) <= row)
                parts.append(jnp.where(counted, 0.0, MASKED).astype(jnp.bfloat16))
            bias = jnp.concatenate(parts, axis=0) if shards > 1 else parts[0]
            masked_keys.append([jnp.concatenate([keys[j], bias], axis=1) for j in range(heads)])
        unit = (
            lax.broadcasted_iota(jnp.int32, (rows, half), 0)
            == lax.broadcasted_iota(jnp.int32, (rows, half), 1)
        )
        unit = jnp.where(unit, 1.0, 0.0).astype(jnp.bfloat16)
        return masked_keys, values, jnp.concatenate([unit] * group, axis=0)

    def scores_of(c, j, keys, units):
        stacked = jnp.concatenate(
            [
                query_ref[c, :, (j * group + g) * half : (j * group + g + 1) * half]
                for g in range(group)
            ],
            axis=0,
        )
        if last:
            stacked = jnp.concatenate([stacked, units], axis=1)
        scores = lax.dot_general(
            stacked, keys[c][j], (((1,), (1,)), ((), ())), preferred_element_type=jnp.float32
        )
        return scores if last else scores + units[c]

    def tiles(scores):
        for i in range(0, scores.shape[1], half):
            yield scores[:, i : min(i + half, scores.shape[1])]

    def compute_near(per_shard):
        keys, values, units = operands(per_shard)
        worst = jnp.zeros((8, half), jnp.float32)
        for c in range(sets):
            for j in range(heads):
                factor = scale_of(j, 0) * LOG2E
                level = state[1][c, j]
                probs = []
                for part in tiles(scores_of(c, j, keys, units)):
                    size = part.shape[1]
                    part = (part - level[:, :size]) * factor[:, :size]
                    probs.append(jnp.exp2(part).astype(jnp.bfloat16))
                weighted = jnp.dot(
                    jnp.concatenate(probs, axis=1), values[j], preferred_element_type=jnp.float32
                )
                total = weighted[:, half:]
                worst = jnp.maximum(worst, jnp.max(total.reshape(stack // 8, 8, half), axis=0))
                total = total + 1.0
                share = pl.reciprocal(total, approx=True)
                share = share * (2.0 - total * share)
                for g in range(group):
                    one = slice(g * rows, (g + 1) * rows)
                    cols = slice((j * group + g) * half, (j * group + g + 1) * half)
                    part = weighted[one, :half] * scale_of(j, 1)
                    part = (part + state[0][c, :, cols].astype(jnp.float32)) * share[one]
                    out_ref[c, :, cols] = part.astype(jnp.bfloat16)
        return jnp.max(worst)

    def compute(per_shard):
        keys, values, units = operands(per_shard)
        for c in range(sets):
            for j in range(heads):
                factor = scale_of(j, 0) * LOG2E
                scores = scores_of(c, j, keys, units)
                top = jnp.max(scores, axis=1, keepdims=True)
                top = jnp.broadcast_to(top, (stack, half))
                if has_state:
                    level = state[1][c, j]
                    top = jnp.maximum(top, level)
                else:
                    top = jnp.maximum(top, FLOOR)
                probs = []
                for part in tiles(scores):
                    size = part.shape[1]
                    part = jnp.exp2((part - top[:, :size]) * factor[:, :size])
                    probs.append(part.astype(jnp.bfloat16))
                weighted = jnp.dot(
                    jnp.concatenate(probs, axis=1), values[j], preferred_element_type=jnp.float32
                )
                acc = weighted[:, :half] * scale_of(j, 1)
                total = weighted[:, half:]
                if has_state:
                    alpha = jnp.exp2((level - top) * factor)
                    total = total + alpha
                else:
                    total = jnp.maximum(total, TINY)
                for g in range(group):
                    one = slice(g * rows, (g + 1) * rows)
                    cols = slice((j * group + g) * half, (j * group + g + 1) * half)
                    part = acc[one]
                    if has_state:
                        part = part + state[0][c, :, cols].astype(jnp.float32) * alpha[one]
                    out_ref[c, :, cols] = (part / total[one]).astype(jnp.bfloat16)
                if not last:
                    level_out[c, j] = top + jnp.log2(total) / factor

    def picked(pick, found):
        own = jnp.concatenate([part for parts in found for part in parts], axis=1)
        return jnp.dot(pick, own, preferred_element_type=jnp.float32)

    if last:

        def deliver(per_shard):
            total = picked(pick_ref[...], per_shard[0]) + moved_ref[...].astype(jnp.float32)
            moved_out[...] = total.astype(jnp.bfloat16)

        latest = bases[0]
        for base in bases[1:]:
            latest = jnp.maximum(latest, base)
        needed = spans[0][0] < latest + rows

        @pl.when(needed)
        def _():
            per_shard = shard_codes()
            worst = compute_near(per_shard)
            deliver(per_shard)

            @pl.when(worst > FAR)
            def _():
                compute(per_shard)

        @pl.when(jnp.logical_not(needed))
        def _():
            deliver(shard_codes())
            out_ref[...] = state[0][...]

    else:
        per_shard = shard_codes()
        compute(per_shard)
        place = place_ref[...]
        total = None
        for (offset, count), found in zip(spans, per_shard):
            part = picked(picker(place, offset, count), found)
            total = part if total is None else total + part
        if with_codes:
            ((offset, count),) = spans_of(count_refs, info_ref, (3,), tokens)
            pick_out[...] = picker(place, offset, count)
        moved_out[...] = total.astype(jnp.bfloat16)


def attend(counts, info, steps, ready, rows, codes=None, state=None, picked=None):
    ints, floats, signs, place, _, query = ready
    tokens, heads, width = rows[0].shape
    half = width // 2
    sets, query_rows, query_width = query.shape
    group = query_width // half // heads
    args = list(counts) if info is None else [info]
    specs = [VMEM_SPEC] * len(counts) if info is None else [SMEM_SPEC]
    args += [ints, floats, signs, query]
    if codes is not None:
        args.append(codes)
    args += rows
    if state is not None:
        args += list(state)
    last = picked is not None
    args += list(picked) if last else [place]
    specs += [VMEM_SPEC] * (len(args) - len(specs))
    outs = [jax.ShapeDtypeStruct(query.shape, jnp.bfloat16)]
    if not last:
        stacked = (sets, heads, group * query_rows, half)
        outs.append(jax.ShapeDtypeStruct(stacked, jnp.float32))
    outs.append(jax.ShapeDtypeStruct((tokens, heads * width), jnp.bfloat16))
    if codes is not None:
        outs.append(jax.ShapeDtypeStruct((tokens, tokens), jnp.bfloat16))
    keys = tokens * len(steps)
    work = sets * heads * group * query_rows * keys
    return pl.pallas_call(
        functools.partial(
            attend_kernel,
            len(counts) if info is None else 0,
            steps,
            codes is not None,
            state is not None,
            last,
        ),
        out_shape=outs,
        in_specs=specs,
        out_specs=[VMEM_SPEC] * len(outs),
        scratch_shapes=[pltpu.VMEM((2, tokens * heads, half), jnp.float32)],
        compiler_params=pltpu.CompilerParams(vmem_limit_bytes=VMEM_LIMIT),
        cost_estimate=pl.CostEstimate(
            flops=work * half * 8, bytes_accessed=4 << 20, transcendentals=work
        ),
    )(*args)


def finish_kernel(
    floats_ref, signs_ref, pick_ref, result_ref, own, other, other_rows, *outs_and_scratch
):
    attention_out, cache_out, rot_scr, cache_scr, sems = outs_and_scratch
    tokens, heads, width = other_rows.shape
    half = width // 2
    sets = result_ref.shape[0]
    rep_id = lax.axis_index("rep")
    sent = [
        pltpu.make_async_copy(result_ref.at[c], attention_out.at[c], sems.at[c]) for c in range(sets)
    ]
    for copy in sent:
        copy.start()
    scales = [scale_reader(floats_ref, side, heads) for side in range(2)]
    found = codes_of(other_rows, scales[1], signs_ref[...], rot_scr)
    both = jnp.concatenate([part for parts in found for part in parts], axis=1)
    pick = pick_ref[...]
    pieces = []
    start = 0
    for i, eighths in enumerate(PIECES):
        size = tokens // 12 * eighths
        here = pl.ds(start, size)
        pieces.append(
            (
                slice(start, start + size),
                pltpu.make_async_copy(cache_scr.at[here], cache_out.at[here], sems.at[sets + i]),
            )
        )
        start += size

    for turn in range(2):

        @pl.when(rep_id == turn)
        def _(turn=turn):
            for here, piece in pieces:
                for side, moved in enumerate((own, other)):
                    first = (side if turn == 0 else 1 - side) * heads
                    if side == 1:
                        added = jnp.dot(pick[here], both, preferred_element_type=jnp.float32)
                    for j in range(heads):
                        for w in range(2):
                            cols = slice((2 * j + w) * half, (2 * j + w + 1) * half)
                            part = moved[here, cols].astype(jnp.float32)
                            if side == 1:
                                part = part + added[:, cols]
                            part = part * scales[side](j, w)
                            cache_scr[here, first + j, w * half : (w + 1) * half] = part
                piece.start()

    for copy in sent + [piece for _, piece in pieces]:
        copy.wait()


def finish(ready, pick, result, own, other, other_rows):
    _, floats, signs, _, _, _ = ready
    tokens, heads, width = other_rows.shape
    cache = (tokens, 2 * heads, width)
    args = [floats, signs, pick, result, own, other, other_rows]
    return pl.pallas_call(
        finish_kernel,
        out_shape=[
            jax.ShapeDtypeStruct(result.shape, result.dtype),
            jax.ShapeDtypeStruct(cache, jnp.float32),
        ],
        in_specs=[VMEM_SPEC] * len(args),
        out_specs=[pl.BlockSpec(memory_space=pl.ANY)] * 2,
        scratch_shapes=[
            pltpu.VMEM((2, tokens * heads, width // 2), jnp.float32),
            pltpu.VMEM(cache, jnp.float32),
            pltpu.SemaphoreType.DMA((result.shape[0] + len(PIECES),)),
        ],
        compiler_params=pltpu.CompilerParams(vmem_limit_bytes=VMEM_LIMIT),
        cost_estimate=pl.CostEstimate(
            flops=tokens * tokens * heads * width * 4, bytes_accessed=2 << 20, transcendentals=0
        ),
    )(*args)


def pair(value, axis, step):
    size = lax.axis_size(axis)
    return lax.ppermute(value, axis, [(i, i ^ step) for i in range(size)])


def body(kv_rows, kv_scales, queries, shard_counts, span_starts, block_slots):
    across = pair(kv_rows, "ctx", 2)
    beside = pair(kv_rows, "ctx", 1)
    ready = make_ready(
        span_starts, kv_scales.T, shard_counts, block_slots[None, :], kv_rows, queries
    )
    count = jnp.broadcast_to(shard_counts[:, None], (8, 128))
    counts = [count, pair(count, "ctx", 1), pair(count, "ctx", 2)]
    corner = pair(across, "ctx", 1)
    *state, moved, pick = attend(counts, None, (0, 1, 2), ready, [beside, across], ready[4])
    moved_other = pair(moved, "rep", 1)
    corner_other = pair(corner, "rep", 1)
    result, own = attend(counts, None, (3,), ready, [corner], None, state, (pick, moved))
    return finish(ready, pick, result, own, moved_other, corner_other)


def body_any(kv_rows, kv_scales, queries, shard_counts, span_starts, block_slots):
    counts = lax.all_gather(shard_counts, "ctx", axis=0, tiled=True)
    info = jnp.stack([jnp.cumsum(counts) - counts, counts], axis=1)
    every = lax.all_gather(kv_rows, "ctx", axis=0)
    size = 4 if every.shape[0] % 4 == 0 else 1
    every = every.reshape(-1, size, *kv_rows.shape)
    info = info.reshape(-1, size, 2)
    ready = make_ready(
        span_starts, kv_scales.T, shard_counts, block_slots[None, :], kv_rows, queries
    )

    def take(some, rows, state=None):
        return attend([], some, (0,) * size, ready, [rows[i] for i in range(size)], None, state)

    def step(carry, turn):
        state, moved = carry
        rows, some = turn
        *state, found = take(some, rows, state)
        return (tuple(state), moved + found), None

    *state, moved = take(info[0], every[0])
    (state, moved), _ = lax.scan(step, (tuple(state), moved), (every[1:], info[1:]))
    none = jnp.zeros((kv_rows.shape[0],) * 2, jnp.bfloat16)
    return finish(ready, none, state[0], moved, pair(moved, "rep", 1), kv_rows)


def solution(mesh):
    in_specs = (
        P(("groups", "ctx"), ("head", "rep"), None),
        P(),
        P(None, ("groups", "ctx"), ("head", "rep")),
        P(("groups", "ctx")),
        P("groups"),
        P("groups"),
    )
    out_specs = (P(None, ("groups", "ctx"), ("head", "rep")), P(("groups", "ctx"), "head", None))
    chosen = body if mesh.shape["ctx"] == 4 else body_any
    return jax.shard_map(chosen, mesh=mesh, in_specs=in_specs, out_specs=out_specs, check_vma=False)
```
